32 devices in a mesh: groups: 2 (over y), enc: 16 (over z, x, core), dp: 1.
Axes of the slice: x: 2, y: 2, z: 4, core: 2. Of those that a mesh axis runs over, the one named last changes fastest.
Arguments:
- tokens: bfloat16 [2, 2048, 1280], P(('groups', 'dp'), 'enc'), parts along dimension 0
- cotangent: bfloat16 [2, 2048, 1280], P(('groups', 'dp'), 'enc'), parts along dimension 0
- page_of_band: int32 [2, 16], P(('groups', 'dp'), 'enc'), parts along dimension 0, may hold values from 0 to 3, never falling along the last dimension, each value on 1 to 5 neighbouring positions
- window_order: int32 [2, 16, 128], P(('groups', 'dp'), 'enc'), parts along dimension 0, may hold values from 0 to 127, each once within a row
- qkv_weight: bfloat16 [2, 1280, 1920], P(None, ('enc', 'dp'))
- out_weight: bfloat16 [2, 640, 1280], P(None, None, ('enc', 'dp')), may hold values from -0.25 to 0.25
- norm_gain: float32 [2, 1280], replicated, may hold values from 0.1 to 1.9
Outputs:
- mixed: bfloat16 [2, 2048, 1280], P(('groups', 'dp'), 'enc'), parts along dimension 0
- grad_tokens: float32 [2, 2048, 1280], P(('groups', 'dp'), 'enc'), parts along dimension 0
- grad_gain: float32 [4, 1280], P('groups'), parts along dimension 0
The draws below stay inside these ranges and needn't reach their ends.
There are 2 independent parts, one for each index of `groups`. The reference program is written for one: setup_inputs(seed, part) draws one part's arguments, and reference() takes and returns one part's arrays. A program takes and returns all parts, laid end to end along the dimension named above; an argument that names none is the same for every part. Nothing has to cross between parts.
Inputs may be any that keep to these rules, and one draw needn't show every extreme that they name: `page_of_band`: along a batch row page numbers never fall; each page covers 1 to 5 consecutive bands, some page exactly 5, and every number up to 3 is used. `window_order`: each band's row lists every position of the band once.
All inputs are finite; a program needn't handle non-finite values.
Results may differ from the reference program's by a relative error of at most 0.029.
Values may be sent and summed in bfloat16 or wider, within the bound.
A program may use at most 128 MiB of HBM per device.

```python
import math
import jax
import jax.numpy as jnp
import numpy as np
from jax import lax

D = 1280
HDIM = 80
HEADS = 8
WIN = 64
BAND = 128
MAXB = 5
HD = 640
BATCH = 1
BANDS = 16
SEQ = 2048
PAGES = 4


def draw_tokens(key, part):
    key = jax.random.fold_in(key, 11)
    full_shape = (BATCH, SEQ, D)
    columns = jnp.exp(jax.random.uniform(jax.random.fold_in(key, 1), (D,), jnp.float32, jnp.log(0.3), jnp.log(3.0)))
    values = jax.random.normal(jax.random.fold_in(key, 2), full_shape, jnp.float32) * columns
    return values.astype(jnp.bfloat16)


def draw_cotangent(key, part):
    key = jax.random.fold_in(key, 23)
    full_shape = (BATCH, SEQ, D)
    rising = 0.4 * 3.0 ** (jnp.arange(SEQ, dtype=jnp.float32) / SEQ)
    rising = rising.reshape(1, SEQ, 1)
    values = jax.random.normal(jax.random.fold_in(key, 1), full_shape, jnp.float32) * rising
    return values.astype(jnp.bfloat16)


def draw_qkv_weight(key, part):
    key = jax.random.fold_in(key, 37)
    columns = HEADS * HDIM
    normal_part = jax.random.normal(jax.random.fold_in(key, 1), (2, D, 3 * columns), jnp.float32) * D ** (-0.5)
    return normal_part.astype(jnp.bfloat16)


def block_scale(key, shape, pieces, low, high):
    def one(axis_at, shards_of):
        draws = jax.random.uniform(jax.random.fold_in(jax.random.fold_in(key, 6), axis_at), (shards_of,), jnp.float32, low / len(pieces), high / len(pieces))
        return jnp.repeat(jnp.exp(draws), shape[axis_at] // shards_of).reshape((-1,) + (1,) * (len(shape) - axis_at - 1))

    gain = one(*pieces[0])
    for cut in pieces[1:]:
        gain = gain * one(*cut)
    return gain


def split_up(count, total, limit, skew):
    weights = [(1 << 20) // math.isqrt(rank ** skew) + 1 for rank in range(2, count + 1)]
    rest, given = total - limit - (count - 1), [1] * (count - 1)
    while rest > 0:
        movable = [i for i in range(count - 1) if given[i] < limit]
        pool, remaining = sum([weights[i] for i in movable]), rest
        for i in movable:
            addition = min(limit - given[i], max(1, remaining * weights[i] // pool), rest)
            given[i] = given[i] + addition
            rest = rest - addition
    return np.array([limit] + given)


def uneven(rng, amount, total, limit, skew):
    if amount == 2:
        one = jax.random.randint(rng, (), max(1, total - limit), min(limit, total - 1) + 1)
        return jnp.stack([one, total - one])
    sizes = jnp.asarray(split_up(amount, total, limit, skew), jnp.int32)
    pairs = (amount - 1) // 2
    giver, taker = sizes[1:1 + 2 * pairs:2], sizes[2:2 + 2 * pairs:2]
    room = jnp.minimum(giver - 1, limit - taker)
    passed = jax.random.randint(jax.random.fold_in(rng, 1), (pairs,), 0, 1 << 20) % (room + 1)
    sizes = sizes.at[1:1 + 2 * pairs:2].set(giver - passed).at[2:2 + 2 * pairs:2].set(taker + passed)
    return sizes[jax.random.permutation(jax.random.fold_in(rng, 2), amount)]


def scatter_about(key, extent, deviation, limit, shards=(), kind=jnp.bfloat16):
    array = jax.random.normal(key, extent, jnp.float32) * deviation
    if len(shards) > 0:
        array = block_scale(key, extent, shards, -0.22, 0.18) * array
    return jnp.clip(array, min=-limit, max=limit).astype(kind)


def setup_inputs(seed: int = 0, part: int = 0) -> dict:
    streams_of = jax.random.split(jax.random.key(seed), 8)
    part_keys = jax.random.split(jax.random.fold_in(streams_of[7], part), 8)
    return {
        "tokens": draw_tokens(jax.random.fold_in(jax.random.fold_in(streams_of[7], part), 71), part),
        "cotangent": draw_cotangent(jax.random.fold_in(jax.random.fold_in(streams_of[7], part), 71), part),
        "page_of_band": jax.vmap(lambda own: jnp.searchsorted(jnp.cumsum(uneven(own, PAGES, BANDS, MAXB, 2)), jnp.arange(BANDS), side="right"))(jax.random.split(part_keys[2], BATCH)).reshape((BATCH, BANDS)).astype(jnp.int32),
        "window_order": jax.vmap(lambda own: jax.random.permutation(own, BAND))(jax.random.split(part_keys[3], BATCH * BANDS)).reshape((BATCH, BANDS, BAND)).astype(jnp.int32),
        "qkv_weight": draw_qkv_weight(jax.random.fold_in(streams_of[7], 71), part),
        "out_weight": scatter_about(streams_of[5], (2, HD, D), HD ** -0.5, 0.25, ((2, 16),)),
        "norm_gain": jnp.clip(1.0 + 0.18 * jax.random.normal(streams_of[6], (2, D), jnp.float32), 0.1, 1.9),
    }


EPSILON = 1e-06
MASKED = -1e+30

def normalize(inputs, gain_row):
    widened = inputs.astype(jnp.float32)
    inverse = lax.rsqrt(lax.optimization_barrier(jnp.mean(widened * widened, axis=-1, keepdims=True)) + EPSILON)
    return ((widened * inverse * gain_row).astype(jnp.bfloat16), inverse)

def norm_back(inputs, gain_row, inverse, grad_normed):
    widened = inputs.astype(jnp.float32)
    scaled = grad_normed * gain_row
    inner = lax.optimization_barrier(jnp.mean(scaled * widened, axis=-1, keepdims=True))
    grad_inputs = inverse * scaled - widened * inverse ** 3 * inner
    grad_row = lax.optimization_barrier(jnp.sum(grad_normed * widened * inverse, axis=0))
    return (grad_inputs, grad_row)

def split_heads(matrix):
    return matrix.reshape(matrix.shape[0], HEADS, HDIM).transpose(1, 0, 2)

def join_heads(stacked):
    return stacked.transpose(1, 0, 2).reshape(stacked.shape[1], -1)

def head_scores(head_query, head_key, allowed):
    factor = head_query.shape[-1] ** (-0.5)
    scores = jnp.dot(head_query, head_key.T, preferred_element_type=jnp.float32) * factor
    return jnp.where(allowed, scores, MASKED)

def attend_forward(queries, keys_all, values_all, allowed):

    def per_head(inputs):
        scores = head_scores(inputs[0], inputs[1], allowed)
        largest = lax.optimization_barrier(jnp.max(scores, axis=-1, keepdims=True))
        logsum = largest + jnp.log(lax.optimization_barrier(jnp.sum(jnp.exp(scores - largest), axis=-1, keepdims=True)))
        probs = jnp.exp(scores - logsum).astype(jnp.bfloat16)
        output = jnp.dot(probs, inputs[2], preferred_element_type=jnp.float32)
        return (output, logsum[:, 0])
    output, logsum = lax.map(per_head, (split_heads(queries), split_heads(keys_all), split_heads(values_all)))
    return (join_heads(output).astype(jnp.bfloat16), logsum)

def head_deltas(output, grad_out):
    return lax.optimization_barrier(jnp.sum(split_heads(grad_out).astype(jnp.float32) * split_heads(output).astype(jnp.float32), axis=-1))

def attend_backward(queries, keys_all, values_all, output, grad_out, logsum, allowed):
    deltas = head_deltas(output, grad_out)

    def per_head(inputs):
        head_query, head_key, head_value, head_grad, head_logsum, head_delta = inputs
        factor = head_query.shape[-1] ** (-0.5)
        scores = head_scores(head_query, head_key, allowed)
        probs = jnp.exp(scores - head_logsum[:, None])
        grad_probs = jnp.dot(head_grad, head_value.T, preferred_element_type=jnp.float32)
        grad_scores = (probs * (grad_probs - head_delta[:, None])).astype(jnp.bfloat16)
        grad_value = jnp.dot(probs.astype(jnp.bfloat16).T, head_grad, preferred_element_type=jnp.float32)
        grad_query = jnp.dot(grad_scores, head_key, preferred_element_type=jnp.float32) * factor
        grad_key = jnp.dot(grad_scores.T, head_query, preferred_element_type=jnp.float32) * factor
        return (grad_query, grad_key, grad_value)
    grads = lax.map(per_head, (split_heads(queries), split_heads(keys_all), split_heads(values_all), split_heads(grad_out), logsum, deltas))
    return (join_heads(grads[0]), join_heads(grads[1]), join_heads(grads[2]))

def padded_band_inputs(keys_all, values_all, tags):
    reach = (MAXB - 1) * BAND
    padded_keys = jnp.pad(keys_all, ((reach, reach), (0, 0)))
    padded_values = jnp.pad(values_all, ((reach, reach), (0, 0)))
    row_tags = jnp.repeat(tags, BAND)
    padded_tags = jnp.pad(row_tags, (reach, reach))
    return (padded_keys, padded_values, row_tags, padded_tags)

def full_forward(queries, keys_all, values_all, tags):
    span = (2 * MAXB - 1) * BAND
    padded_keys, padded_values, row_tags, padded_tags = padded_band_inputs(keys_all, values_all, tags)

    def one_band(first):
        band_queries = lax.dynamic_slice_in_dim(queries, first, BAND, 0)
        near_keys = lax.dynamic_slice_in_dim(padded_keys, first, span, 0)
        near_values = lax.dynamic_slice_in_dim(padded_values, first, span, 0)
        allowed = lax.dynamic_slice_in_dim(row_tags, first, BAND, 0)[:, None] == lax.dynamic_slice_in_dim(padded_tags, first, span, 0)[None, :]
        return attend_forward(band_queries, near_keys, near_values, allowed)
    firsts = jnp.arange(BANDS, dtype=jnp.int32) * BAND
    output, logsum = lax.map(one_band, firsts)
    return (output.reshape(SEQ, -1), logsum)

def full_backward(queries, keys_all, values_all, output, grad_out, logsum, tags):
    span = (2 * MAXB - 1) * BAND
    reach = (MAXB - 1) * BAND
    padded_keys, padded_values, row_tags, padded_tags = padded_band_inputs(keys_all, values_all, tags)

    def one_band(carried, inputs):
        first, band_logsum = inputs
        grad_keys_pad, grad_values_pad = carried
        band_queries = lax.dynamic_slice_in_dim(queries, first, BAND, 0)
        band_output = lax.dynamic_slice_in_dim(output, first, BAND, 0)
        band_grad = lax.dynamic_slice_in_dim(grad_out, first, BAND, 0)
        near_keys = lax.dynamic_slice_in_dim(padded_keys, first, span, 0)
        near_values = lax.dynamic_slice_in_dim(padded_values, first, span, 0)
        allowed = lax.dynamic_slice_in_dim(row_tags, first, BAND, 0)[:, None] == lax.dynamic_slice_in_dim(padded_tags, first, span, 0)[None, :]
        grad_query, grad_key, grad_value = attend_backward(band_queries, near_keys, near_values, band_output, band_grad, band_logsum, allowed)
        grad_keys_pad = lax.dynamic_update_slice_in_dim(grad_keys_pad, lax.dynamic_slice_in_dim(grad_keys_pad, first, span, 0) + grad_key, first, 0)
        grad_values_pad = lax.dynamic_update_slice_in_dim(grad_values_pad, lax.dynamic_slice_in_dim(grad_values_pad, first, span, 0) + grad_value, first, 0)
        return ((grad_keys_pad, grad_values_pad), grad_query)
    zeros = jnp.zeros(padded_keys.shape, jnp.float32)
    firsts = jnp.arange(BANDS, dtype=jnp.int32) * BAND
    carried, grad_queries = lax.scan(one_band, (zeros, zeros), (firsts, logsum))
    return (grad_queries.reshape(SEQ, -1), carried[0][reach:reach + SEQ], carried[1][reach:reach + SEQ])

def window_forward(queries, keys_all, values_all, order):
    allowed = jnp.ones((WIN, WIN), dtype=jnp.bool_)

    def one_window(window_query, window_key, window_value):
        return attend_forward(window_query, window_key, window_value, allowed)

    def one_band(inputs):
        band_order = inputs[3]
        grouped = [matrix[band_order].reshape(BAND // WIN, WIN, -1) for matrix in inputs[:3]]
        output, logsum = jax.vmap(one_window)(grouped[0], grouped[1], grouped[2])
        restored = jnp.zeros((BAND, output.shape[-1]), jnp.bfloat16).at[band_order].set(output.reshape(BAND, -1))
        return (restored, logsum)
    banded = [matrix.reshape(BANDS, BAND, -1) for matrix in (queries, keys_all, values_all)]
    output, logsum = lax.map(one_band, (banded[0], banded[1], banded[2], order))
    return (output.reshape(SEQ, -1), logsum)

def window_backward(queries, keys_all, values_all, output, grad_out, logsum, order):
    allowed = jnp.ones((WIN, WIN), dtype=jnp.bool_)

    def one_window(window_query, window_key, window_value, window_output, window_grad, window_logsum):
        return attend_backward(window_query, window_key, window_value, window_output, window_grad, window_logsum, allowed)

    def one_band(inputs):
        band_order = inputs[5]
        grouped = [matrix[band_order].reshape(BAND // WIN, WIN, -1) for matrix in inputs[:5]]
        grads = jax.vmap(one_window)(grouped[0], grouped[1], grouped[2], grouped[3], grouped[4], inputs[6])
        return tuple((jnp.zeros((BAND, grad.shape[-1]), jnp.float32).at[band_order].set(grad.reshape(BAND, -1)) for grad in grads))
    banded = [matrix.reshape(BANDS, BAND, -1) for matrix in (queries, keys_all, values_all, output, grad_out)]
    grads = lax.map(one_band, (banded[0], banded[1], banded[2], banded[3], banded[4], order, logsum))
    return tuple((grad.reshape(SEQ, -1) for grad in grads))

def reference(tokens, cotangent, page_of_band, window_order, qkv_weight, out_weight, norm_gain):

    def one_row(inputs):
        inputs_row, grad_mixed, tags, order = inputs
        normed_full, inverse_full = normalize(inputs_row, norm_gain[0])
        packed_full = jnp.dot(normed_full, qkv_weight[0], preferred_element_type=jnp.float32).astype(jnp.bfloat16)
        query_full = packed_full[:, :HD]
        key_full = packed_full[:, HD:2 * HD]
        value_full = packed_full[:, 2 * HD:]
        att_full, logsum_full = full_forward(query_full, key_full, value_full, tags)
        hidden = (inputs_row.astype(jnp.float32) + jnp.dot(att_full, out_weight[0], preferred_element_type=jnp.float32)).astype(jnp.bfloat16)
        normed_window, inverse_window = normalize(hidden, norm_gain[1])
        packed_window = jnp.dot(normed_window, qkv_weight[1], preferred_element_type=jnp.float32).astype(jnp.bfloat16)
        query_window = packed_window[:, :HD]
        key_window = packed_window[:, HD:2 * HD]
        value_window = packed_window[:, 2 * HD:]
        att_window, logsum_window = window_forward(query_window, key_window, value_window, order)
        mixed = (hidden.astype(jnp.float32) + jnp.dot(att_window, out_weight[1], preferred_element_type=jnp.float32)).astype(jnp.bfloat16)
        dout_window = jnp.dot(grad_mixed, out_weight[1].T, preferred_element_type=jnp.float32).astype(jnp.bfloat16)
        grads_window = window_backward(query_window, key_window, value_window, att_window, dout_window, logsum_window, order)
        dpacked_window = jnp.concatenate(grads_window, axis=-1).astype(jnp.bfloat16)
        dnormed_window = jnp.dot(dpacked_window, qkv_weight[1].T, preferred_element_type=jnp.float32)
        hidden_part, gain_window = norm_back(hidden, norm_gain[1], inverse_window, dnormed_window)
        dhidden = grad_mixed.astype(jnp.float32) + hidden_part
        dout_full = jnp.dot(dhidden.astype(jnp.bfloat16), out_weight[0].T, preferred_element_type=jnp.float32).astype(jnp.bfloat16)
        grads_full = full_backward(query_full, key_full, value_full, att_full, dout_full, logsum_full, tags)
        dpacked_full = jnp.concatenate(grads_full, axis=-1).astype(jnp.bfloat16)
        dnormed_full = jnp.dot(dpacked_full, qkv_weight[0].T, preferred_element_type=jnp.float32)
        tokens_part, gain_full = norm_back(inputs_row, norm_gain[0], inverse_full, dnormed_full)
        return (mixed, dhidden + tokens_part, jnp.stack([gain_full, gain_window]))
    mixed, grad_tokens, gains = lax.map(one_row, (tokens, cotangent, page_of_band + 1, window_order))
    return (mixed, grad_tokens, lax.optimization_barrier(jnp.sum(gains, axis=0)))
```

```python
import functools

import jax
import jax.numpy as jnp
from jax import lax
from jax.experimental import pallas as pl
from jax.experimental.pallas import tpu as pltpu
from jax.sharding import PartitionSpec as P

HDIM = 80
HEADS = 8
WIN = 64
MAXB = 5
REACH = MAXB - 1
SLOTS = 2 * REACH + 1
EPSILON = 1e-06
MASKED = -1e30
FACTOR = HDIM**-0.5
OFFSETS = [d for k in range(REACH, 0, -1) for d in (k, -k)]
MESH = pl.DeviceIdType.MESH
VMEM = pl.BlockSpec(memory_space=pltpu.VMEM)
SMEM = pl.BlockSpec(memory_space=pltpu.SMEM)
LIMIT = 48 * 1024 * 1024
F32 = jnp.float32
BF16 = jnp.bfloat16


def mm(a, b):
    return jnp.dot(a, b, preferred_element_type=F32)


def mt(a, b):
    return lax.dot_general(a, b, (((1,), (1,)), ((), ())), preferred_element_type=F32)


def tm(a, b):
    return lax.dot_general(a, b, (((0,), (0,)), ((), ())), preferred_element_type=F32)


def normalize(x, gain_row):
    inverse = lax.rsqrt(jnp.mean(x * x, axis=-1, keepdims=True) + EPSILON)
    return (x * inverse * gain_row).astype(BF16), inverse


def norm_back(x, gain_row, inverse, grad_normed):
    scaled = grad_normed * gain_row
    inner = jnp.mean(scaled * x, axis=-1, keepdims=True)
    grad_inputs = inverse * scaled - x * (inverse * inverse * inverse) * inner
    grad_row = jnp.sum(grad_normed * (x * inverse), axis=0, keepdims=True)
    return grad_inputs, grad_row


def halo_kernel(count, *refs):
    n = lax.axis_size("enc")
    ins, outs = refs[:count], refs[count : 2 * count]
    send, recv = refs[2 * count :]
    me = lax.axis_index("enc")
    barrier = pltpu.get_barrier_semaphore()

    def valid(d):
        return me + d < n if d > 0 else me + d >= 0

    def copy(a, d, source, slot):
        return pltpu.make_async_remote_copy(
            src_ref=source,
            dst_ref=outs[a].at[slot],
            send_sem=send.at[a, REACH + d],
            recv_sem=recv.at[a, slot],
            device_id={"enc": me + d},
            device_id_type=MESH,
        )

    for d in OFFSETS:

        @pl.when(valid(d))
        def _():
            pl.semaphore_signal(barrier, inc=1, device_id={"enc": me + d}, device_id_type=MESH)

    pl.semaphore_wait(barrier, jnp.minimum(me, REACH) + jnp.minimum(n - 1 - me, REACH))

    for d in OFFSETS:

        @pl.when(valid(d))
        def _():
            for a in range(count):
                copy(a, d, ins[a], REACH - d).start()

    for a in range(count):
        outs[a][REACH] = ins[a][...]
    for d in OFFSETS:

        @pl.when(jnp.logical_not(valid(d)))
        def _():
            for a in range(count):
                outs[a][REACH + d] = jnp.zeros(ins[a].shape, ins[a].dtype)

    for d in OFFSETS:

        @pl.when(valid(d))
        def _():
            for a in range(count):
                copy(a, d, ins[a], REACH - d).wait_send()
                copy(a, d, ins[a], REACH + d).wait_recv()


def halo(collective_id, *arrays):
    count = len(arrays)
    return pl.pallas_call(
        functools.partial(halo_kernel, count),
        out_shape=[jax.ShapeDtypeStruct((SLOTS,) + a.shape, a.dtype) for a in arrays],
        in_specs=[VMEM] * count,
        out_specs=[VMEM] * count,
        scratch_shapes=[
            pltpu.SemaphoreType.DMA((count, SLOTS)),
            pltpu.SemaphoreType.DMA((count, SLOTS)),
        ],
        compiler_params=pltpu.CompilerParams(
            collective_id=collective_id, has_side_effects=True, vmem_limit_bytes=LIMIT
        ),
    )(*arrays)


def total_kernel(row_ref, out_ref, held, send, recv):
    n, m = lax.axis_size("enc"), lax.axis_size("dp")
    total = n * m
    me = lax.axis_index("enc") * m + lax.axis_index("dp")
    barrier = pltpu.get_barrier_semaphore()

    def peer(o):
        t = lax.rem(me + o, total)
        return {"enc": t // m, "dp": lax.rem(t, m)}

    def copy(o):
        return pltpu.make_async_remote_copy(
            src_ref=row_ref,
            dst_ref=held.at[o],
            send_sem=send.at[o],
            recv_sem=recv.at[o],
            device_id=peer(o),
            device_id_type=MESH,
        )

    def greet(o, c):
        pl.semaphore_signal(barrier, inc=1, device_id=peer(o), device_id_type=MESH)
        return c

    def begin(o, c):
        copy(o).start()
        return c

    def finish(o, c):
        copy(o).wait()
        return c

    lax.fori_loop(1, total, greet, 0)
    pl.semaphore_wait(barrier, total - 1)
    lax.fori_loop(1, total, begin, 0)
    held[0] = row_ref[...]
    lax.fori_loop(1, total, finish, 0)

    out_ref[...] = lax.fori_loop(1, total, lambda o, s: s + held[o], held[0])


def total_rows(rows):
    total = lax.axis_size("enc") * lax.axis_size("dp")
    return pl.pallas_call(
        total_kernel,
        out_shape=jax.ShapeDtypeStruct(rows.shape, rows.dtype),
        in_specs=[VMEM],
        out_specs=VMEM,
        scratch_shapes=[
            pltpu.VMEM((total,) + rows.shape, rows.dtype),
            pltpu.SemaphoreType.DMA((total,)),
            pltpu.SemaphoreType.DMA((total,)),
        ],
        compiler_params=pltpu.CompilerParams(
            collective_id=2, has_side_effects=True, vmem_limit_bytes=LIMIT
        ),
    )(rows)


def first_slot(tags):
    first = REACH
    for s in range(REACH - 1, -1, -1):
        first = jnp.where(tags[s] == tags[REACH], s, first)
    return first


def band_mask(tags, first, band):
    lanes = lax.broadcasted_iota(jnp.int32, (1, MAXB * band), 1)
    mask = lanes < 0
    for j in range(MAXB):
        same = (tags[first + j] == tags[REACH]).astype(jnp.int32)
        inside = jnp.logical_and(lanes >= j * band, lanes < (j + 1) * band)
        mask = jnp.logical_or(mask, jnp.logical_and(inside, same == 1))
    return mask


def full_kernel(tags, near, weight, gain, packed, att, lse, hidden):
    band = near.shape[1]
    cols = HEADS * HDIM
    first = first_slot(tags)
    mask = band_mask(tags, first, band)
    for j in range(MAXB):
        x = near[first + j].astype(F32)
        normed, _ = normalize(x, gain[0:1, :])
        for c in range(3):
            packed[j * band : (j + 1) * band, c * cols : (c + 1) * cols] = mm(
                normed, weight[:, c * cols : (c + 1) * cols]
            ).astype(BF16)
    own = pl.ds(pl.multiple_of((REACH - first) * band, band), band)
    queries = packed[own, 0:cols]
    lses = []
    for h in range(HEADS):
        a, b = h * HDIM, (h + 1) * HDIM
        scores = mt(queries[:, a:b], packed[:, cols + a : cols + b]) * FACTOR
        scores = jnp.where(mask, scores, MASKED)
        largest = jnp.max(scores, axis=-1, keepdims=True)
        raw = jnp.exp(scores - largest)
        summed = jnp.sum(raw, axis=-1, keepdims=True)
        probs = (raw * (1.0 / summed)).astype(BF16)
        att[:, a:b] = mm(probs, packed[:, 2 * cols + a : 2 * cols + b]).astype(BF16)
        lses.append(largest + jnp.log(summed))
    lse[...] = jnp.concatenate(lses, axis=1)
    hidden[...] = (near[REACH].astype(F32) + mt(att[...], weight[:, 3 * cols :])).astype(BF16)


def window_kernel(
    hidden_ref, cot_ref, same, weight, full_out, gain, att_full, lse_full,
    mixed, dhidden_ref, dout_full, stats, gain_row, packed, att, dpacked,
):
    cols = HEADS * HDIM
    x = hidden_ref[...].astype(F32)
    normed, inverse = normalize(x, gain[1:2, :])
    for c in range(3):
        packed[:, c * cols : (c + 1) * cols] = mm(
            normed, weight[:, c * cols : (c + 1) * cols]
        ).astype(BF16)
    cot = cot_ref[...]
    out_t = weight[:, 3 * cols :]
    dout = mm(cot, out_t).astype(BF16)
    mask = same[...] > 0.5
    for h in range(HEADS):
        a, b = h * HDIM, (h + 1) * HDIM
        q, k = packed[:, a:b], packed[:, cols + a : cols + b]
        v, g = packed[:, 2 * cols + a : 2 * cols + b], dout[:, a:b]
        scores = jnp.where(mask, mt(q, k) * FACTOR, MASKED)
        largest = jnp.max(scores, axis=-1, keepdims=True)
        raw = jnp.exp(scores - largest)
        p = raw * (1.0 / jnp.sum(raw, axis=-1, keepdims=True))
        probs = p.astype(BF16)
        out = mm(probs, v).astype(BF16)
        att[:, a:b] = out
        delta = jnp.sum(g.astype(F32) * out.astype(F32), axis=-1, keepdims=True)
        ds = (p * (mt(g, v) - delta)).astype(BF16)
        dpacked[:, a:b] = (mm(ds, k) * FACTOR).astype(BF16)
        dpacked[:, cols + a : cols + b] = (tm(ds, q) * FACTOR).astype(BF16)
        dpacked[:, 2 * cols + a : 2 * cols + b] = tm(probs, g).astype(BF16)
    mixed[...] = (x + mt(att[...], out_t)).astype(BF16)
    dnormed = mt(dpacked[...], weight[:, : 3 * cols])
    part, row = norm_back(x, gain[1:2, :], inverse, dnormed)
    gain_row[...] = row
    dhidden = cot.astype(F32) + part
    dhidden_ref[...] = dhidden
    dfull = mm(dhidden.astype(BF16), full_out[:, 3 * cols :]).astype(BF16)
    dout_full[...] = dfull
    product = dfull.astype(F32) * att_full[...].astype(F32)
    columns = [lse_full[...]] + [
        jnp.sum(product[:, h * HDIM : (h + 1) * HDIM], axis=-1, keepdims=True)
        for h in range(HEADS)
    ]
    columns.append(jnp.zeros((x.shape[0], 128 - 2 * HEADS), F32))
    stats[...] = jnp.concatenate(columns, axis=1).T[: 2 * HEADS]


def back_kernel(
    tags, packed, near_dout, near_stats, tokens, dhidden, weight, gain,
    grad_tokens, gain_row, dpacked,
):
    band = tokens.shape[0]
    cols = HEADS * HDIM
    first = first_slot(tags)
    mask = band_mask(tags, first, band)
    own = pl.ds(pl.multiple_of((REACH - first) * band, band), band)
    mine = packed[own, :]
    own_stats = near_stats[REACH].T
    gout = jnp.concatenate([near_dout[first + j] for j in range(MAXB)], axis=0)
    rows = jnp.concatenate([near_stats[first + j] for j in range(MAXB)], axis=1)
    own_out = near_dout[REACH]
    for h in range(HEADS):
        a, b = h * HDIM, (h + 1) * HDIM
        q, k, v = mine[:, a:b], mine[:, cols + a : cols + b], mine[:, 2 * cols + a : 2 * cols + b]
        g = own_out[:, a:b]
        near_q = packed[:, a:b]
        near_k = packed[:, cols + a : cols + b]
        near_v = packed[:, 2 * cols + a : 2 * cols + b]
        near_g = gout[:, a:b]
        scores = jnp.where(mask, mt(q, near_k) * FACTOR, MASKED)
        p = jnp.exp(scores - own_stats[:, h : h + 1])
        ds = (p * (mt(g, near_v) - own_stats[:, HEADS + h : HEADS + h + 1])).astype(BF16)
        dpacked[:, a:b] = (mm(ds, near_k) * FACTOR).astype(BF16)
        scores_t = jnp.where(mask, mt(k, near_q) * FACTOR - rows[h : h + 1, :], MASKED)
        pt = jnp.exp(scores_t)
        dst = (pt * (mt(v, near_g) - rows[HEADS + h : HEADS + h + 1, :])).astype(BF16)
        dpacked[:, cols + a : cols + b] = (mm(dst, near_q) * FACTOR).astype(BF16)
        dpacked[:, 2 * cols + a : 2 * cols + b] = mm(pt.astype(BF16), near_g).astype(BF16)
    dnormed = mt(dpacked[...], weight[:, : 3 * cols])
    x = tokens[...].astype(F32)
    inverse = lax.rsqrt(jnp.mean(x * x, axis=-1, keepdims=True) + EPSILON)
    part, row = norm_back(x, gain[0:1, :], inverse, dnormed)
    gain_row[...] = row
    grad_tokens[...] = dhidden[...] + part


def call(kernel, shapes, in_specs, scratch, flops, *args):
    return pl.pallas_call(
        kernel,
        out_shape=[jax.ShapeDtypeStruct(s, t) for s, t in shapes],
        in_specs=in_specs,
        out_specs=[VMEM] * len(shapes),
        scratch_shapes=scratch,
        compiler_params=pltpu.CompilerParams(vmem_limit_bytes=LIMIT),
        cost_estimate=pl.CostEstimate(flops=flops, bytes_accessed=8 << 20, transcendentals=1 << 20),
    )(*args)


def shards(tokens, cotangent, page_of_band, window_order, qkv_weight, out_weight, norm_gain):
    x = tokens[0]
    band, width = x.shape
    cols = HEADS * HDIM
    wide = 3 * cols
    weights = [
        lax.all_gather(
            jnp.concatenate([qkv_weight[i], out_weight[i].T], axis=1),
            ("enc", "dp"), axis=0, tiled=True,
        )
        for i in range(2)
    ]
    tag = jnp.broadcast_to((page_of_band + 1).astype(F32), (8, 128))
    near, near_tag = halo(0, x, tag)
    tags = near_tag[:, 0, 0].astype(jnp.int32)
    order = window_order[0, 0]
    late = jnp.arange(band)[:, None] >= WIN
    side = jnp.any((order[:, None] == jnp.arange(band)[None, :]) & late, axis=0)
    same = (side[:, None] == side[None, :]).astype(F32)
    packed, att, lse, hidden = call(
        full_kernel,
        [((MAXB * band, wide), BF16), ((band, cols), BF16), ((band, HEADS), F32), ((band, width), BF16)],
        [SMEM, VMEM, VMEM, VMEM], [], 6 << 30,
        tags, near, weights[0], norm_gain,
    )
    mixed, dhidden, dout, stats, row_window = call(
        window_kernel,
        [((band, width), BF16), ((band, width), F32), ((band, cols), BF16), ((2 * HEADS, band), F32), ((1, width), F32)],
        [VMEM] * 8,
        [pltpu.VMEM((band, wide), BF16), pltpu.VMEM((band, cols), BF16), pltpu.VMEM((band, wide), BF16)],
        3 << 30,
        hidden, cotangent[0], same, weights[1], weights[0], norm_gain, att, lse,
    )
    near_dout, near_stats = halo(1, dout, stats)
    grad_tokens, row_full = call(
        back_kernel,
        [((band, width), F32), ((1, width), F32)],
        [SMEM] + [VMEM] * 7,
        [pltpu.VMEM((band, wide), BF16)],
        3 << 30,
        tags, packed, near_dout, near_stats, x, dhidden, weights[0], norm_gain,
    )
    grad_gain = total_rows(jnp.concatenate([row_full, row_window], axis=0))
    return mixed[None], grad_tokens[None], grad_gain


def solution(mesh):
    return jax.shard_map(
        shards,
        mesh=mesh,
        in_specs=(
            P(("groups", "dp"), "enc", None),
            P(("groups", "dp"), "enc", None),
            P(("groups", "dp"), "enc"),
            P(("groups", "dp"), "enc", None),
            P(None, ("enc", "dp"), None),
            P(None, None, ("enc", "dp")),
            P(),
        ),
        out_specs=(
            P(("groups", "dp"), "enc", None),
            P(("groups", "dp"), "enc", None),
            P("groups", None),
        ),
        check_vma=False,
    )
```

```python
import functools

import jax
import jax.numpy as jnp
from jax import lax
from jax.experimental import pallas as pl
from jax.experimental.pallas import tpu as pltpu
from jax.sharding import PartitionSpec as P

HDIM = 80
HEADS = 8
WIN = 64
MAXB = 5
REACH = MAXB - 1
SLOTS = 2 * REACH + 1
EPSILON = 1e-06
MASKED = -1e30
FACTOR = HDIM**-0.5
OFFSETS = [d for k in range(REACH, 0, -1) for d in (k, -k)]
MESH = pl.DeviceIdType.MESH
VMEM = pl.BlockSpec(memory_space=pltpu.VMEM)
SMEM = pl.BlockSpec(memory_space=pltpu.SMEM)
LIMIT = 48 * 1024 * 1024
F32 = jnp.float32
BF16 = jnp.bfloat16


def mm(a, b):
    return jnp.dot(a, b, preferred_element_type=F32)


def mt(a, b):
    return lax.dot_general(a, b, (((1,), (1,)), ((), ())), preferred_element_type=F32)


def tm(a, b):
    return lax.dot_general(a, b, (((0,), (0,)), ((), ())), preferred_element_type=F32)


def normalize(x, gain_row):
    inverse = lax.rsqrt(jnp.mean(x * x, axis=-1, keepdims=True) + EPSILON)
    return (x * inverse * gain_row).astype(BF16), inverse


def norm_back(x, gain_row, inverse, grad_normed):
    scaled = grad_normed * gain_row
    inner = jnp.mean(scaled * x, axis=-1, keepdims=True)
    grad_inputs = inverse * scaled - x * (inverse * inverse * inverse) * inner
    grad_row = jnp.sum(grad_normed * (x * inverse), axis=0, keepdims=True)
    return grad_inputs, grad_row


def halo_kernel(count, *refs):
    n = lax.axis_size("enc")
    ins, outs = refs[:count], refs[count : 2 * count]
    send, recv = refs[2 * count :]
    me = lax.axis_index("enc")
    barrier = pltpu.get_barrier_semaphore()

    def valid(d):
        return me + d < n if d > 0 else me + d >= 0

    def copy(a, d, source, slot):
        return pltpu.make_async_remote_copy(
            src_ref=source,
            dst_ref=outs[a].at[slot],
            send_sem=send.at[a, REACH + d],
            recv_sem=recv.at[a, slot],
            device_id={"enc": me + d},
            device_id_type=MESH,
        )

    for d in OFFSETS:

        @pl.when(valid(d))
        def _():
            pl.semaphore_signal(barrier, inc=1, device_id={"enc": me + d}, device_id_type=MESH)

    pl.semaphore_wait(barrier, jnp.minimum(me, REACH) + jnp.minimum(n - 1 - me, REACH))

    for d in OFFSETS:

        @pl.when(valid(d))
        def _():
            for a in range(count):
                copy(a, d, ins[a], REACH - d).start()

    for a in range(count):
        outs[a][REACH] = ins[a][...]
    for d in OFFSETS:

        @pl.when(jnp.logical_not(valid(d)))
        def _():
            for a in range(count):
                outs[a][REACH + d] = jnp.zeros(ins[a].shape, ins[a].dtype)

    for d in OFFSETS:

        @pl.when(valid(d))
        def _():
            for a in range(count):
                copy(a, d, ins[a], REACH - d).wait_send()
                copy(a, d, ins[a], REACH + d).wait_recv()


def halo(collective_id, *arrays):
    count = len(arrays)
    return pl.pallas_call(
        functools.partial(halo_kernel, count),
        out_shape=[jax.ShapeDtypeStruct((SLOTS,) + a.shape, a.dtype) for a in arrays],
        in_specs=[VMEM] * count,
        out_specs=[VMEM] * count,
        scratch_shapes=[
            pltpu.SemaphoreType.DMA((count, SLOTS)),
            pltpu.SemaphoreType.DMA((count, SLOTS)),
        ],
        compiler_params=pltpu.CompilerParams(
            collective_id=collective_id, has_side_effects=True, vmem_limit_bytes=LIMIT
        ),
    )(*arrays)


def gather_halo_kernel(count, *refs):
    n = lax.axis_size("enc")
    weight, ins, full, outs = refs[0], refs[1 : 1 + count], refs[1 + count], refs[2 + count : 2 + 2 * count]
    send, recv, shard_send, shard_recv = refs[2 + 2 * count :]
    me = lax.axis_index("enc")
    barrier = pltpu.get_barrier_semaphore()
    planes = n // 4
    z = me // 4
    across = me + 2 - 4 * (lax.rem(me, 4) // 2)
    other = me + 1 - 2 * lax.rem(me, 2)

    def valid(d):
        return me + d < n if d > 0 else me + d >= 0

    def copy(a, d, source, slot):
        return pltpu.make_async_remote_copy(
            src_ref=source,
            dst_ref=outs[a].at[slot],
            send_sem=send.at[a, REACH + d],
            recv_sem=recv.at[a, slot],
            device_id={"enc": me + d},
            device_id_type=MESH,
        )

    def shard(s, to, k, source=None):
        return pltpu.make_async_remote_copy(
            src_ref=full.at[s] if source is None else source,
            dst_ref=full.at[s],
            send_sem=shard_send.at[s, k],
            recv_sem=shard_recv.at[s],
            device_id={"enc": to},
            device_id_type=MESH,
        )

    for d in OFFSETS:

        @pl.when(valid(d))
        def _():
            pl.semaphore_signal(barrier, inc=1, device_id={"enc": me + d}, device_id_type=MESH)

    pl.semaphore_wait(barrier, jnp.minimum(me, REACH) + jnp.minimum(n - 1 - me, REACH))

    @pl.when(z + 1 < planes)
    def _():
        shard(me, me + 4, 0, weight).start()

    @pl.when(z > 0)
    def _():
        shard(me, me - 4, 1, weight).start()

    shard(me, across, 2, weight).start()
    shard(me, other, 3, weight).start()
    for d in OFFSETS:

        @pl.when(valid(d))
        def _():
            for a in range(count):
                copy(a, d, ins[a], REACH - d).start()

    full[me] = weight[...]
    for a in range(count):
        outs[a][REACH] = ins[a][...]
    for d in OFFSETS:

        @pl.when(jnp.logical_not(valid(d)))
        def _():
            for a in range(count):
                outs[a][REACH + d] = jnp.zeros(ins[a].shape, ins[a].dtype)

    def present(step):
        return z + step < planes if step > 0 else z + step >= 0

    for distance in range(1, planes + 1):
        if distance < planes:
            for step in (-distance, distance):

                @pl.when(present(step))
                def _():
                    s = me + 4 * step
                    shard(s, other, 3).wait_recv()
                    back = -1 if step > 0 else 1

                    @pl.when(present(back))
                    def _():
                        shard(s, me + 4 * back, 0).start()

                    shard(s, across, 2).start()
                    shard(s, other, 3).start()

        for step in sorted({1 - distance, distance - 1}):

            @pl.when(present(step))
            def _():
                s = across + 4 * step
                shard(s, other, 3).wait_recv()
                shard(s, other, 3).start()

    for plane in range(planes):
        for x in range(2):
            s = 4 * plane + 2 * x + lax.rem(other, 2)
            shard(s, other, 3).wait_recv()

    for d in OFFSETS:

        @pl.when(valid(d))
        def _():
            for a in range(count):
                copy(a, d, ins[a], REACH - d).wait_send()
                copy(a, d, ins[a], REACH + d).wait_recv()

    @pl.when(z + 1 < planes)
    def _():
        shard(me, me + 4, 0, weight).wait_send()

    @pl.when(z > 0)
    def _():
        shard(me, me - 4, 1, weight).wait_send()

    shard(me, across, 2, weight).wait_send()
    shard(me, other, 3, weight).wait_send()
    for distance in range(planes):
        for step in sorted({-distance, distance}):

            @pl.when(present(step))
            def _():
                s = me + 4 * step
                if distance > 0:
                    back = -1 if step > 0 else 1

                    @pl.when(present(back))
                    def _():
                        shard(s, me + 4 * back, 0).wait_send()

                    shard(s, across, 2).wait_send()
                    shard(s, other, 3).wait_send()
                shard(across + 4 * step, other, 3).wait_send()


def gather_halo(weight, *arrays):
    count = len(arrays)
    n = lax.axis_size("enc")
    return pl.pallas_call(
        functools.partial(gather_halo_kernel, count),
        out_shape=[jax.ShapeDtypeStruct((n,) + weight.shape, weight.dtype)]
        + [jax.ShapeDtypeStruct((SLOTS,) + a.shape, a.dtype) for a in arrays],
        in_specs=[VMEM] * (count + 1),
        out_specs=[VMEM] * (count + 1),
        scratch_shapes=[
            pltpu.SemaphoreType.DMA((count, SLOTS)),
            pltpu.SemaphoreType.DMA((count, SLOTS)),
            pltpu.SemaphoreType.DMA((n, 4)),
            pltpu.SemaphoreType.DMA((n,)),
        ],
        compiler_params=pltpu.CompilerParams(
            collective_id=0, has_side_effects=True, vmem_limit_bytes=LIMIT
        ),
    )(weight, *arrays)


def total_kernel(row_ref, out_ref, held, send, recv):
    n, m = lax.axis_size("enc"), lax.axis_size("dp")
    total = n * m
    me = lax.axis_index("enc") * m + lax.axis_index("dp")
    barrier = pltpu.get_barrier_semaphore()

    def peer(o):
        t = lax.rem(me + o, total)
        return {"enc": t // m, "dp": lax.rem(t, m)}

    def copy(o):
        return pltpu.make_async_remote_copy(
            src_ref=row_ref,
            dst_ref=held.at[o],
            send_sem=send.at[o],
            recv_sem=recv.at[o],
            device_id=peer(o),
            device_id_type=MESH,
        )

    def greet(o, c):
        pl.semaphore_signal(barrier, inc=1, device_id=peer(o), device_id_type=MESH)
        return c

    def begin(o, c):
        copy(o).start()
        return c

    def finish(o, c):
        copy(o).wait()
        return c

    lax.fori_loop(1, total, greet, 0)
    pl.semaphore_wait(barrier, total - 1)
    lax.fori_loop(1, total, begin, 0)
    held[0] = row_ref[...]
    lax.fori_loop(1, total, finish, 0)

    out_ref[...] = lax.fori_loop(1, total, lambda o, s: s + held[o], held[0])


def total_rows(rows):
    total = lax.axis_size("enc") * lax.axis_size("dp")
    return pl.pallas_call(
        total_kernel,
        out_shape=jax.ShapeDtypeStruct(rows.shape, rows.dtype),
        in_specs=[VMEM],
        out_specs=VMEM,
        scratch_shapes=[
            pltpu.VMEM((total,) + rows.shape, rows.dtype),
            pltpu.SemaphoreType.DMA((total,)),
            pltpu.SemaphoreType.DMA((total,)),
        ],
        compiler_params=pltpu.CompilerParams(
            collective_id=2, has_side_effects=True, vmem_limit_bytes=LIMIT
        ),
    )(rows)


def first_slot(tags):
    first = REACH
    for s in range(REACH - 1, -1, -1):
        first = jnp.where(tags[s] == tags[REACH], s, first)
    return first


def band_mask(tags, first, band):
    lanes = lax.broadcasted_iota(jnp.int32, (1, MAXB * band), 1)
    mask = lanes < 0
    for j in range(MAXB):
        same = (tags[first + j] == tags[REACH]).astype(jnp.int32)
        inside = jnp.logical_and(lanes >= j * band, lanes < (j + 1) * band)
        mask = jnp.logical_or(mask, jnp.logical_and(inside, same == 1))
    return mask


def full_kernel(tags, near, weight, gain, packed, att, lse, hidden):
    band = near.shape[1]
    cols = HEADS * HDIM
    first = first_slot(tags)
    mask = band_mask(tags, first, band)
    for j in range(MAXB):
        x = near[first + j].astype(F32)
        normed, _ = normalize(x, gain[0:1, :])
        for c in range(3):
            packed[j * band : (j + 1) * band, c * cols : (c + 1) * cols] = mm(
                normed, weight[:, c * cols : (c + 1) * cols]
            ).astype(BF16)
    own = pl.ds(pl.multiple_of((REACH - first) * band, band), band)
    queries = packed[own, 0:cols]
    lses = []
    for h in range(HEADS):
        a, b = h * HDIM, (h + 1) * HDIM
        scores = mt(queries[:, a:b], packed[:, cols + a : cols + b]) * FACTOR
        scores = jnp.where(mask, scores, MASKED)
        largest = jnp.max(scores, axis=-1, keepdims=True)
        raw = jnp.exp(scores - largest)
        summed = jnp.sum(raw, axis=-1, keepdims=True)
        probs = (raw * (1.0 / summed)).astype(BF16)
        att[:, a:b] = mm(probs, packed[:, 2 * cols + a : 2 * cols + b]).astype(BF16)
        lses.append(largest + jnp.log(summed))
    lse[...] = jnp.concatenate(lses, axis=1)
    hidden[...] = (near[REACH].astype(F32) + mt(att[...], weight[:, 3 * cols :])).astype(BF16)


def window_kernel(
    hidden_ref, cot_ref, same, weight, full_out, gain, att_full, lse_full,
    mixed, dhidden_ref, dout_full, stats, gain_row, packed, att, dpacked,
):
    cols = HEADS * HDIM
    x = hidden_ref[...].astype(F32)
    normed, inverse = normalize(x, gain[1:2, :])
    for c in range(3):
        packed[:, c * cols : (c + 1) * cols] = mm(
            normed, weight[:, c * cols : (c + 1) * cols]
        ).astype(BF16)
    cot = cot_ref[...]
    out_t = weight[:, 3 * cols :]
    dout = mm(cot, out_t).astype(BF16)
    mask = same[...] > 0.5
    for h in range(HEADS):
        a, b = h * HDIM, (h + 1) * HDIM
        q, k = packed[:, a:b], packed[:, cols + a : cols + b]
        v, g = packed[:, 2 * cols + a : 2 * cols + b], dout[:, a:b]
        scores = jnp.where(mask, mt(q, k) * FACTOR, MASKED)
        largest = jnp.max(scores, axis=-1, keepdims=True)
        raw = jnp.exp(scores - largest)
        p = raw * (1.0 / jnp.sum(raw, axis=-1, keepdims=True))
        probs = p.astype(BF16)
        out = mm(probs, v).astype(BF16)
        att[:, a:b] = out
        delta = jnp.sum(g.astype(F32) * out.astype(F32), axis=-1, keepdims=True)
        ds = (p * (mt(g, v) - delta)).astype(BF16)
        dpacked[:, a:b] = (mm(ds, k) * FACTOR).astype(BF16)
        dpacked[:, cols + a : cols + b] = (tm(ds, q) * FACTOR).astype(BF16)
        dpacked[:, 2 * cols + a : 2 * cols + b] = tm(probs, g).astype(BF16)
    mixed[...] = (x + mt(att[...], out_t)).astype(BF16)
    dnormed = mt(dpacked[...], weight[:, : 3 * cols])
    part, row = norm_back(x, gain[1:2, :], inverse, dnormed)
    gain_row[...] = row
    dhidden = cot.astype(F32) + part
    dhidden_ref[...] = dhidden
    dfull = mm(dhidden.astype(BF16), full_out[:, 3 * cols :]).astype(BF16)
    dout_full[...] = dfull
    product = dfull.astype(F32) * att_full[...].astype(F32)
    columns = [lse_full[...]] + [
        jnp.sum(product[:, h * HDIM : (h + 1) * HDIM], axis=-1, keepdims=True)
        for h in range(HEADS)
    ]
    columns.append(jnp.zeros((x.shape[0], 128 - 2 * HEADS), F32))
    stats[...] = jnp.concatenate(columns, axis=1).T[: 2 * HEADS]


def back_kernel(
    tags, packed, near_dout, near_stats, tokens, dhidden, weight, gain,
    grad_tokens, gain_row, dpacked,
):
    band = tokens.shape[0]
    cols = HEADS * HDIM
    first = first_slot(tags)
    mask = band_mask(tags, first, band)
    own = pl.ds(pl.multiple_of((REACH - first) * band, band), band)
    mine = packed[own, :]
    own_stats = near_stats[REACH].T
    gout = jnp.concatenate([near_dout[first + j] for j in range(MAXB)], axis=0)
    rows = jnp.concatenate([near_stats[first + j] for j in range(MAXB)], axis=1)
    own_out = near_dout[REACH]
    for h in range(HEADS):
        a, b = h * HDIM, (h + 1) * HDIM
        q, k, v = mine[:, a:b], mine[:, cols + a : cols + b], mine[:, 2 * cols + a : 2 * cols + b]
        g = own_out[:, a:b]
        near_q = packed[:, a:b]
        near_k = packed[:, cols + a : cols + b]
        near_v = packed[:, 2 * cols + a : 2 * cols + b]
        near_g = gout[:, a:b]
        scores = jnp.where(mask, mt(q, near_k) * FACTOR, MASKED)
        p = jnp.exp(scores - own_stats[:, h : h + 1])
        ds = (p * (mt(g, near_v) - own_stats[:, HEADS + h : HEADS + h + 1])).astype(BF16)
        dpacked[:, a:b] = (mm(ds, near_k) * FACTOR).astype(BF16)
        scores_t = jnp.where(mask, mt(k, near_q) * FACTOR - rows[h : h + 1, :], MASKED)
        pt = jnp.exp(scores_t)
        dst = (pt * (mt(v, near_g) - rows[HEADS + h : HEADS + h + 1, :])).astype(BF16)
        dpacked[:, cols + a : cols + b] = (mm(dst, near_q) * FACTOR).astype(BF16)
        dpacked[:, 2 * cols + a : 2 * cols + b] = mm(pt.astype(BF16), near_g).astype(BF16)
    dnormed = mt(dpacked[...], weight[:, : 3 * cols])
    x = tokens[...].astype(F32)
    inverse = lax.rsqrt(jnp.mean(x * x, axis=-1, keepdims=True) + EPSILON)
    part, row = norm_back(x, gain[0:1, :], inverse, dnormed)
    gain_row[...] = row
    grad_tokens[...] = dhidden[...] + part


def call(kernel, shapes, in_specs, scratch, flops, *args):
    return pl.pallas_call(
        kernel,
        out_shape=[jax.ShapeDtypeStruct(s, t) for s, t in shapes],
        in_specs=in_specs,
        out_specs=[VMEM] * len(shapes),
        scratch_shapes=scratch,
        compiler_params=pltpu.CompilerParams(vmem_limit_bytes=LIMIT),
        cost_estimate=pl.CostEstimate(flops=flops, bytes_accessed=8 << 20, transcendentals=1 << 20),
    )(*args)


def shards(tokens, cotangent, page_of_band, window_order, qkv_weight, out_weight, norm_gain):
    x = tokens[0]
    band, width = x.shape
    cols = HEADS * HDIM
    wide = 3 * cols
    pieces = [jnp.concatenate([qkv_weight[i], out_weight[i].T], axis=1) for i in range(2)]
    tag = jnp.broadcast_to((page_of_band + 1).astype(F32), (8, 128))
    gathers = lax.axis_size("dp") == 1 and lax.axis_size("enc") % 4 == 0 and pieces[0].shape[0] % 16 == 0
    weights = [
        None if gathers and i == 0 else lax.all_gather(pieces[i], ("enc", "dp"), axis=0, tiled=True)
        for i in range(2)
    ]
    if gathers:
        full, near, near_tag = gather_halo(pieces[0], x, tag)
        weights[0] = full.reshape(width, pieces[0].shape[1])
    else:
        near, near_tag = halo(0, x, tag)
    tags = near_tag[:, 0, 0].astype(jnp.int32)
    order = window_order[0, 0]
    late = jnp.arange(band)[:, None] >= WIN
    side = jnp.any((order[:, None] == jnp.arange(band)[None, :]) & late, axis=0)
    same = (side[:, None] == side[None, :]).astype(F32)
    packed, att, lse, hidden = call(
        full_kernel,
        [((MAXB * band, wide), BF16), ((band, cols), BF16), ((band, HEADS), F32), ((band, width), BF16)],
        [SMEM, VMEM, VMEM, VMEM], [], 6 << 30,
        tags, near, weights[0], norm_gain,
    )
    mixed, dhidden, dout, stats, row_window = call(
        window_kernel,
        [((band, width), BF16), ((band, width), F32), ((band, cols), BF16), ((2 * HEADS, band), F32), ((1, width), F32)],
        [VMEM] * 8,
        [pltpu.VMEM((band, wide), BF16), pltpu.VMEM((band, cols), BF16), pltpu.VMEM((band, wide), BF16)],
        3 << 30,
        hidden, cotangent[0], same, weights[1], weights[0], norm_gain, att, lse,
    )
    near_dout, near_stats = halo(1, dout, stats)
    grad_tokens, row_full = call(
        back_kernel,
        [((band, width), F32), ((1, width), F32)],
        [SMEM] + [VMEM] * 7,
        [pltpu.VMEM((band, wide), BF16)],
        3 << 30,
        tags, packed, near_dout, near_stats, x, dhidden, weights[0], norm_gain,
    )
    grad_gain = total_rows(jnp.concatenate([row_full, row_window], axis=0))
    return mixed[None], grad_tokens[None], grad_gain


def solution(mesh):
    return jax.shard_map(
        shards,
        mesh=mesh,
        in_specs=(
            P(("groups", "dp"), "enc", None),
            P(("groups", "dp"), "enc", None),
            P(("groups", "dp"), "enc"),
            P(("groups", "dp"), "enc", None),
            P(None, ("enc", "dp"), None),
            P(None, None, ("enc", "dp")),
            P(),
        ),
        out_specs=(
            P(("groups", "dp"), "enc", None),
            P(("groups", "dp"), "enc", None),
            P("groups", None),
        ),
        check_vma=False,
    )
```

```python
import functools

import jax
import jax.numpy as jnp
from jax import lax
from jax.experimental import pallas as pl
from jax.experimental.pallas import tpu as pltpu
from jax.sharding import PartitionSpec as P

HDIM = 80
HEADS = 8
WIN = 64
MAXB = 5
REACH = MAXB - 1
SLOTS = 2 * REACH + 1
EPSILON = 1e-06
MASKED = -1e30
FACTOR = HDIM**-0.5
OFFSETS = [d for k in range(REACH, 0, -1) for d in (k, -k)]
MESH = pl.DeviceIdType.MESH
VMEM = pl.BlockSpec(memory_space=pltpu.VMEM)
SMEM = pl.BlockSpec(memory_space=pltpu.SMEM)
LIMIT = 48 * 1024 * 1024
F32 = jnp.float32
BF16 = jnp.bfloat16


def mm(a, b):
    return jnp.dot(a, b, preferred_element_type=F32)


def mt(a, b):
    return lax.dot_general(a, b, (((1,), (1,)), ((), ())), preferred_element_type=F32)


def tm(a, b):
    return lax.dot_general(a, b, (((0,), (0,)), ((), ())), preferred_element_type=F32)


def normalize(x, gain_row):
    inverse = lax.rsqrt(jnp.mean(x * x, axis=-1, keepdims=True) + EPSILON)
    return (x * inverse * gain_row).astype(BF16), inverse


def norm_back(x, gain_row, inverse, grad_normed):
    scaled = grad_normed * gain_row
    inner = jnp.mean(scaled * x, axis=-1, keepdims=True)
    grad_inputs = inverse * scaled - x * (inverse * inverse * inverse) * inner
    grad_row = jnp.sum(grad_normed * (x * inverse), axis=0, keepdims=True)
    return grad_inputs, grad_row


def halo_kernel(count, *refs):
    n = lax.axis_size("enc")
    ins, outs = refs[:count], refs[count : 2 * count]
    send, recv = refs[2 * count :]
    me = lax.axis_index("enc")
    barrier = pltpu.get_barrier_semaphore()

    def valid(d):
        return me + d < n if d > 0 else me + d >= 0

    def copy(a, d, source, slot):
        return pltpu.make_async_remote_copy(
            src_ref=source,
            dst_ref=outs[a].at[slot],
            send_sem=send.at[a, REACH + d],
            recv_sem=recv.at[a, slot],
            device_id={"enc": me + d},
            device_id_type=MESH,
        )

    for d in OFFSETS:

        @pl.when(valid(d))
        def _():
            pl.semaphore_signal(barrier, inc=1, device_id={"enc": me + d}, device_id_type=MESH)

    pl.semaphore_wait(barrier, jnp.minimum(me, REACH) + jnp.minimum(n - 1 - me, REACH))

    for d in OFFSETS:

        @pl.when(valid(d))
        def _():
            for a in range(count):
                copy(a, d, ins[a], REACH - d).start()

    for a in range(count):
        outs[a][REACH] = ins[a][...]
    for d in OFFSETS:

        @pl.when(jnp.logical_not(valid(d)))
        def _():
            for a in range(count):
                outs[a][REACH + d] = jnp.zeros(ins[a].shape, ins[a].dtype)

    for d in OFFSETS:

        @pl.when(valid(d))
        def _():
            for a in range(count):
                copy(a, d, ins[a], REACH - d).wait_send()
                copy(a, d, ins[a], REACH + d).wait_recv()


def halo(collective_id, *arrays):
    count = len(arrays)
    return pl.pallas_call(
        functools.partial(halo_kernel, count),
        out_shape=[jax.ShapeDtypeStruct((SLOTS,) + a.shape, a.dtype) for a in arrays],
        in_specs=[VMEM] * count,
        out_specs=[VMEM] * count,
        scratch_shapes=[
            pltpu.SemaphoreType.DMA((count, SLOTS)),
            pltpu.SemaphoreType.DMA((count, SLOTS)),
        ],
        compiler_params=pltpu.CompilerParams(
            collective_id=collective_id, has_side_effects=True, vmem_limit_bytes=LIMIT
        ),
    )(*arrays)


def gather_halo_kernel(count, *refs):
    n = lax.axis_size("enc")
    pieces, ins, fulls = refs[:2], refs[2 : 2 + count], refs[2 + count : 4 + count]
    outs = refs[4 + count : 4 + 2 * count]
    send, recv, shard_send, shard_recv = refs[4 + 2 * count :]
    me, group = lax.axis_index("enc"), lax.axis_index("groups")
    half = pieces[0].shape[1] // 2
    barrier = pltpu.get_barrier_semaphore()
    planes = n // 4
    z = me // 4
    across = me + 2 - 4 * (lax.rem(me, 4) // 2)
    other = me + 1 - 2 * lax.rem(me, 2)
    sent = []

    def valid(d):
        return me + d < n if d > 0 else me + d >= 0

    def present(*steps):
        good = z >= 0
        for step in steps:
            good = jnp.logical_and(good, z + step < planes if step > 0 else z + step >= 0)
        return good

    def copy(a, d, source, slot):
        return pltpu.make_async_remote_copy(
            src_ref=source,
            dst_ref=outs[a].at[slot],
            send_sem=send.at[a, REACH + d],
            recv_sem=recv.at[a, slot],
            device_id={"enc": me + d},
            device_id_type=MESH,
        )

    def shard(s, part, k, device, source=None):
        if part is None:
            dst, unit = fulls[0].at[s], 0
        else:
            columns = pl.ds(pl.multiple_of(part * half, half), half)
            dst, unit = fulls[1].at[s, :, columns], 1 + part
            if source is not None:
                source = source.at[:, columns]
        return pltpu.make_async_remote_copy(
            src_ref=dst if source is None else source,
            dst_ref=dst,
            send_sem=shard_send.at[s, unit, k],
            recv_sem=shard_recv.at[s, unit],
            device_id=device,
            device_id_type=MESH,
        )

    core, side, twin = {"enc": other}, {"enc": across}, {"groups": 1 - group}

    def begin(steps, s, part, k, device, source=None):
        sent.append((steps, s, part, k, device, source))

        @pl.when(present(*steps))
        def _():
            shard(s, part, k, device, source).start()

    def arrive(steps, s, part):
        @pl.when(present(*steps))
        def _():
            shard(s, part, 3, core).wait_recv()

    for d in OFFSETS:

        @pl.when(valid(d))
        def _():
            pl.semaphore_signal(barrier, inc=1, device_id={"enc": me + d}, device_id_type=MESH)

    pl.semaphore_signal(barrier, inc=1, device_id=twin, device_id_type=MESH)
    pl.semaphore_wait(barrier, jnp.minimum(me, REACH) + jnp.minimum(n - 1 - me, REACH) + 1)

    for part, piece in ((None, pieces[0]), (group, pieces[1])):
        begin((1,), me, part, 0, {"enc": me + 4}, piece)
        begin((-1,), me, part, 1, {"enc": me - 4}, piece)
        begin((), me, part, 2, side, piece)
        begin((), me, part, 3, core, piece)
    begin((), me, 1 - group, 3, core, pieces[1])
    for d in OFFSETS:

        @pl.when(valid(d))
        def _():
            for a in range(count):
                copy(a, d, ins[a], REACH - d).start()

    for f in range(2):
        fulls[f][me] = pieces[f][...]
    for a in range(count):
        outs[a][REACH] = ins[a][...]
    for d in OFFSETS:

        @pl.when(jnp.logical_not(valid(d)))
        def _():
            for a in range(count):
                outs[a][REACH + d] = jnp.zeros(ins[a].shape, ins[a].dtype)

    def steps_at(distance):
        return sorted({-distance, distance}) if 0 <= distance < planes else []

    for distance in range(1, planes + 2):
        for part in (None, group):
            for step in steps_at(distance):
                s, back = me + 4 * step, -1 if step > 0 else 1
                arrive((step,), s, part)
                begin((step, back), s, part, 0, {"enc": me + 4 * back})
                begin((step,), s, part, 2, side)
                begin((step,), s, part, 3, core)
                if part is not None:
                    begin((step,), s, part, 4, twin)
        for part in (None, group):
            for step in steps_at(distance - 1):
                s = across + 4 * step
                arrive((step,), s, part)
                begin((step,), s, part, 3, core)
                if part is not None:
                    begin((step,), s, part, 4, twin)
        lines = [(step, me + 4 * step) for step in steps_at(distance - 1) if step]
        lines += [(step, across + 4 * step) for step in steps_at(distance - 2)]
        for step, s in lines:
            arrive((step,), s, 1 - group)
            begin((step,), s, 1 - group, 3, core)

    for plane in range(planes):
        for x in range(2):
            s = 4 * plane + 2 * x + lax.rem(other, 2)
            for part in (None, 0, 1):
                arrive((), s, part)

    for d in OFFSETS:

        @pl.when(valid(d))
        def _():
            for a in range(count):
                copy(a, d, ins[a], REACH - d).wait_send()
                copy(a, d, ins[a], REACH + d).wait_recv()

    for steps, *rest in sent:

        @pl.when(present(*steps))
        def _():
            shard(*rest).wait_send()


def gather_halo(pieces, *arrays):
    count = len(arrays)
    n = lax.axis_size("enc")
    return pl.pallas_call(
        functools.partial(gather_halo_kernel, count),
        out_shape=[jax.ShapeDtypeStruct((n,) + p.shape, p.dtype) for p in pieces]
        + [jax.ShapeDtypeStruct((SLOTS,) + a.shape, a.dtype) for a in arrays],
        in_specs=[VMEM] * (count + 2),
        out_specs=[VMEM] * (count + 2),
        scratch_shapes=[
            pltpu.SemaphoreType.DMA((count, SLOTS)),
            pltpu.SemaphoreType.DMA((count, SLOTS)),
            pltpu.SemaphoreType.DMA((n, 3, 5)),
            pltpu.SemaphoreType.DMA((n, 3)),
        ],
        compiler_params=pltpu.CompilerParams(
            collective_id=0, has_side_effects=True, vmem_limit_bytes=LIMIT
        ),
    )(*pieces, *arrays)


def total_kernel(row_ref, out_ref, held, send, recv):
    n, m = lax.axis_size("enc"), lax.axis_size("dp")
    total = n * m
    me = lax.axis_index("enc") * m + lax.axis_index("dp")
    barrier = pltpu.get_barrier_semaphore()

    def peer(o):
        t = lax.rem(me + o, total)
        return {"enc": t // m, "dp": lax.rem(t, m)}

    def copy(o):
        return pltpu.make_async_remote_copy(
            src_ref=row_ref,
            dst_ref=held.at[o],
            send_sem=send.at[o],
            recv_sem=recv.at[o],
            device_id=peer(o),
            device_id_type=MESH,
        )

    def greet(o, c):
        pl.semaphore_signal(barrier, inc=1, device_id=peer(o), device_id_type=MESH)
        return c

    def begin(o, c):
        copy(o).start()
        return c

    def finish(o, c):
        copy(o).wait()
        return c

    lax.fori_loop(1, total, greet, 0)
    pl.semaphore_wait(barrier, total - 1)
    lax.fori_loop(1, total, begin, 0)
    held[0] = row_ref[...]
    lax.fori_loop(1, total, finish, 0)

    out_ref[...] = lax.fori_loop(1, total, lambda o, s: s + held[o], held[0])


def total_rows(rows):
    total = lax.axis_size("enc") * lax.axis_size("dp")
    return pl.pallas_call(
        total_kernel,
        out_shape=jax.ShapeDtypeStruct(rows.shape, rows.dtype),
        in_specs=[VMEM],
        out_specs=VMEM,
        scratch_shapes=[
            pltpu.VMEM((total,) + rows.shape, rows.dtype),
            pltpu.SemaphoreType.DMA((total,)),
            pltpu.SemaphoreType.DMA((total,)),
        ],
        compiler_params=pltpu.CompilerParams(
            collective_id=2, has_side_effects=True, vmem_limit_bytes=LIMIT
        ),
    )(rows)


def first_slot(tags):
    first = REACH
    for s in range(REACH - 1, -1, -1):
        first = jnp.where(tags[s] == tags[REACH], s, first)
    return first


def band_mask(tags, first, band):
    lanes = lax.broadcasted_iota(jnp.int32, (1, MAXB * band), 1)
    mask = lanes < 0
    for j in range(MAXB):
        same = (tags[first + j] == tags[REACH]).astype(jnp.int32)
        inside = jnp.logical_and(lanes >= j * band, lanes < (j + 1) * band)
        mask = jnp.logical_or(mask, jnp.logical_and(inside, same == 1))
    return mask


def full_kernel(tags, near, weight, gain, packed, att, lse, hidden):
    band = near.shape[1]
    cols = HEADS * HDIM
    first = first_slot(tags)
    mask = band_mask(tags, first, band)
    for j in range(MAXB):
        x = near[first + j].astype(F32)
        normed, _ = normalize(x, gain[0:1, :])
        for c in range(3):
            packed[j * band : (j + 1) * band, c * cols : (c + 1) * cols] = mm(
                normed, weight[:, c * cols : (c + 1) * cols]
            ).astype(BF16)
    own = pl.ds(pl.multiple_of((REACH - first) * band, band), band)
    queries = packed[own, 0:cols]
    lses = []
    for h in range(HEADS):
        a, b = h * HDIM, (h + 1) * HDIM
        scores = mt(queries[:, a:b], packed[:, cols + a : cols + b]) * FACTOR
        scores = jnp.where(mask, scores, MASKED)
        largest = jnp.max(scores, axis=-1, keepdims=True)
        raw = jnp.exp(scores - largest)
        summed = jnp.sum(raw, axis=-1, keepdims=True)
        probs = (raw * (1.0 / summed)).astype(BF16)
        att[:, a:b] = mm(probs, packed[:, 2 * cols + a : 2 * cols + b]).astype(BF16)
        lses.append(largest + jnp.log(summed))
    lse[...] = jnp.concatenate(lses, axis=1)
    hidden[...] = (near[REACH].astype(F32) + mt(att[...], weight[:, 3 * cols :])).astype(BF16)


def window_kernel(
    hidden_ref, cot_ref, same, weight, full_out, gain, att_full, lse_full,
    mixed, dhidden_ref, dout_full, stats, gain_row, packed, att, dpacked,
):
    cols = HEADS * HDIM
    x = hidden_ref[...].astype(F32)
    normed, inverse = normalize(x, gain[1:2, :])
    for c in range(3):
        packed[:, c * cols : (c + 1) * cols] = mm(
            normed, weight[:, c * cols : (c + 1) * cols]
        ).astype(BF16)
    cot = cot_ref[...]
    out_t = weight[:, 3 * cols :]
    dout = mm(cot, out_t).astype(BF16)
    mask = same[...] > 0.5
    for h in range(HEADS):
        a, b = h * HDIM, (h + 1) * HDIM
        q, k = packed[:, a:b], packed[:, cols + a : cols + b]
        v, g = packed[:, 2 * cols + a : 2 * cols + b], dout[:, a:b]
        scores = jnp.where(mask, mt(q, k) * FACTOR, MASKED)
        largest = jnp.max(scores, axis=-1, keepdims=True)
        raw = jnp.exp(scores - largest)
        p = raw * (1.0 / jnp.sum(raw, axis=-1, keepdims=True))
        probs = p.astype(BF16)
        out = mm(probs, v).astype(BF16)
        att[:, a:b] = out
        delta = jnp.sum(g.astype(F32) * out.astype(F32), axis=-1, keepdims=True)
        ds = (p * (mt(g, v) - delta)).astype(BF16)
        dpacked[:, a:b] = (mm(ds, k) * FACTOR).astype(BF16)
        dpacked[:, cols + a : cols + b] = (tm(ds, q) * FACTOR).astype(BF16)
        dpacked[:, 2 * cols + a : 2 * cols + b] = tm(probs, g).astype(BF16)
    mixed[...] = (x + mt(att[...], out_t)).astype(BF16)
    dnormed = mt(dpacked[...], weight[:, : 3 * cols])
    part, row = norm_back(x, gain[1:2, :], inverse, dnormed)
    gain_row[...] = row
    dhidden = cot.astype(F32) + part
    dhidden_ref[...] = dhidden
    dfull = mm(dhidden.astype(BF16), full_out[:, 3 * cols :]).astype(BF16)
    dout_full[...] = dfull
    product = dfull.astype(F32) * att_full[...].astype(F32)
    columns = [lse_full[...]] + [
        jnp.sum(product[:, h * HDIM : (h + 1) * HDIM], axis=-1, keepdims=True)
        for h in range(HEADS)
    ]
    columns.append(jnp.zeros((x.shape[0], 128 - 2 * HEADS), F32))
    stats[...] = jnp.concatenate(columns, axis=1).T[: 2 * HEADS]


def back_kernel(
    tags, packed, near_dout, near_stats, tokens, dhidden, weight, gain,
    grad_tokens, gain_row, dpacked,
):
    band = tokens.shape[0]
    cols = HEADS * HDIM
    first = first_slot(tags)
    mask = band_mask(tags, first, band)
    own = pl.ds(pl.multiple_of((REACH - first) * band, band), band)
    mine = packed[own, :]
    own_stats = near_stats[REACH].T
    gout = jnp.concatenate([near_dout[first + j] for j in range(MAXB)], axis=0)
    rows = jnp.concatenate([near_stats[first + j] for j in range(MAXB)], axis=1)
    own_out = near_dout[REACH]
    for h in range(HEADS):
        a, b = h * HDIM, (h + 1) * HDIM
        q, k, v = mine[:, a:b], mine[:, cols + a : cols + b], mine[:, 2 * cols + a : 2 * cols + b]
        g = own_out[:, a:b]
        near_q = packed[:, a:b]
        near_k = packed[:, cols + a : cols + b]
        near_v = packed[:, 2 * cols + a : 2 * cols + b]
        near_g = gout[:, a:b]
        scores = jnp.where(mask, mt(q, near_k) * FACTOR, MASKED)
        p = jnp.exp(scores - own_stats[:, h : h + 1])
        ds = (p * (mt(g, near_v) - own_stats[:, HEADS + h : HEADS + h + 1])).astype(BF16)
        dpacked[:, a:b] = (mm(ds, near_k) * FACTOR).astype(BF16)
        scores_t = jnp.where(mask, mt(k, near_q) * FACTOR - rows[h : h + 1, :], MASKED)
        pt = jnp.exp(scores_t)
        dst = (pt * (mt(v, near_g) - rows[HEADS + h : HEADS + h + 1, :])).astype(BF16)
        dpacked[:, cols + a : cols + b] = (mm(dst, near_q) * FACTOR).astype(BF16)
        dpacked[:, 2 * cols + a : 2 * cols + b] = mm(pt.astype(BF16), near_g).astype(BF16)
    dnormed = mt(dpacked[...], weight[:, : 3 * cols])
    x = tokens[...].astype(F32)
    inverse = lax.rsqrt(jnp.mean(x * x, axis=-1, keepdims=True) + EPSILON)
    part, row = norm_back(x, gain[0:1, :], inverse, dnormed)
    gain_row[...] = row
    grad_tokens[...] = dhidden[...] + part


def call(kernel, shapes, in_specs, scratch, flops, *args):
    return pl.pallas_call(
        kernel,
        out_shape=[jax.ShapeDtypeStruct(s, t) for s, t in shapes],
        in_specs=in_specs,
        out_specs=[VMEM] * len(shapes),
        scratch_shapes=scratch,
        compiler_params=pltpu.CompilerParams(vmem_limit_bytes=LIMIT),
        cost_estimate=pl.CostEstimate(flops=flops, bytes_accessed=8 << 20, transcendentals=1 << 20),
    )(*args)


def shards(tokens, cotangent, page_of_band, window_order, qkv_weight, out_weight, norm_gain):
    x = tokens[0]
    band, width = x.shape
    cols = HEADS * HDIM
    wide = 3 * cols
    pieces = [jnp.concatenate([qkv_weight[i], out_weight[i].T], axis=1) for i in range(2)]
    tag = jnp.broadcast_to((page_of_band + 1).astype(F32), (8, 128))
    gathers = lax.axis_size("dp") == 1 and lax.axis_size("groups") == 2
    gathers = gathers and lax.axis_size("enc") % 4 == 0 and pieces[0].shape[0] % 16 == 0
    if gathers:
        *fulls, near, near_tag = gather_halo(pieces, x, tag)
        weights = [full.reshape(width, full.shape[2]) for full in fulls]
    else:
        weights = [lax.all_gather(p, ("enc", "dp"), axis=0, tiled=True) for p in pieces]
        near, near_tag = halo(0, x, tag)
    tags = near_tag[:, 0, 0].astype(jnp.int32)
    order = window_order[0, 0]
    late = jnp.arange(band)[:, None] >= WIN
    side = jnp.any((order[:, None] == jnp.arange(band)[None, :]) & late, axis=0)
    same = (side[:, None] == side[None, :]).astype(F32)
    packed, att, lse, hidden = call(
        full_kernel,
        [((MAXB * band, wide), BF16), ((band, cols), BF16), ((band, HEADS), F32), ((band, width), BF16)],
        [SMEM, VMEM, VMEM, VMEM], [], 6 << 30,
        tags, near, weights[0], norm_gain,
    )
    mixed, dhidden, dout, stats, row_window = call(
        window_kernel,
        [((band, width), BF16), ((band, width), F32), ((band, cols), BF16), ((2 * HEADS, band), F32), ((1, width), F32)],
        [VMEM] * 8,
        [pltpu.VMEM((band, wide), BF16), pltpu.VMEM((band, cols), BF16), pltpu.VMEM((band, wide), BF16)],
        3 << 30,
        hidden, cotangent[0], same, weights[1], weights[0], norm_gain, att, lse,
    )
    near_dout, near_stats = halo(1, dout, stats)
    grad_tokens, row_full = call(
        back_kernel,
        [((band, width), F32), ((1, width), F32)],
        [SMEM] + [VMEM] * 7,
        [pltpu.VMEM((band, wide), BF16)],
        3 << 30,
        tags, packed, near_dout, near_stats, x, dhidden, weights[0], norm_gain,
    )
    grad_gain = total_rows(jnp.concatenate([row_full, row_window], axis=0))
    return mixed[None], grad_tokens[None], grad_gain


def solution(mesh):
    return jax.shard_map(
        shards,
        mesh=mesh,
        in_specs=(
            P(("groups", "dp"), "enc", None),
            P(("groups", "dp"), "enc", None),
            P(("groups", "dp"), "enc"),
            P(("groups", "dp"), "enc", None),
            P(None, ("enc", "dp"), None),
            P(None, None, ("enc", "dp")),
            P(),
        ),
        out_specs=(
            P(("groups", "dp"), "enc", None),
            P(("groups", "dp"), "enc", None),
            P("groups", None),
        ),
        check_vma=False,
    )
```

```python
import functools

import jax
import jax.numpy as jnp
from jax import lax
from jax.experimental import pallas as pl
from jax.experimental.pallas import tpu as pltpu
from jax.sharding import PartitionSpec as P

HDIM = 80
HEADS = 8
WIN = 64
MAXB = 5
REACH = MAXB - 1
SLOTS = 2 * REACH + 1
EPSILON = 1e-06
MASKED = -1e30
FACTOR = HDIM**-0.5
OFFSETS = [d for k in range(REACH, 0, -1) for d in (k, -k)]
MESH = pl.DeviceIdType.MESH
VMEM = pl.BlockSpec(memory_space=pltpu.VMEM)
SMEM = pl.BlockSpec(memory_space=pltpu.SMEM)
LIMIT = 48 * 1024 * 1024
F32 = jnp.float32
BF16 = jnp.bfloat16


def mm(a, b):
    return jnp.dot(a, b, preferred_element_type=F32)


def mt(a, b):
    return lax.dot_general(a, b, (((1,), (1,)), ((), ())), preferred_element_type=F32)


def tm(a, b):
    return lax.dot_general(a, b, (((0,), (0,)), ((), ())), preferred_element_type=F32)


def normalize(x, gain_row):
    inverse = lax.rsqrt(jnp.mean(x * x, axis=-1, keepdims=True) + EPSILON)
    return (x * inverse * gain_row).astype(BF16), inverse


def norm_back(x, gain_row, inverse, grad_normed):
    scaled = grad_normed * gain_row
    inner = jnp.mean(scaled * x, axis=-1, keepdims=True)
    grad_inputs = inverse * scaled - x * (inverse * inverse * inverse) * inner
    grad_row = jnp.sum(grad_normed * (x * inverse), axis=0, keepdims=True)
    return grad_inputs, grad_row


def halo_kernel(count, *refs):
    n = lax.axis_size("enc")
    ins, outs = refs[:count], refs[count : 2 * count]
    send, recv = refs[2 * count :]
    me = lax.axis_index("enc")
    barrier = pltpu.get_barrier_semaphore()

    def valid(d):
        return me + d < n if d > 0 else me + d >= 0

    def copy(a, d, source, slot):
        return pltpu.make_async_remote_copy(
            src_ref=source,
            dst_ref=outs[a].at[slot],
            send_sem=send.at[a, REACH + d],
            recv_sem=recv.at[a, slot],
            device_id={"enc": me + d},
            device_id_type=MESH,
        )

    for d in OFFSETS:

        @pl.when(valid(d))
        def _():
            pl.semaphore_signal(barrier, inc=1, device_id={"enc": me + d}, device_id_type=MESH)

    pl.semaphore_wait(barrier, jnp.minimum(me, REACH) + jnp.minimum(n - 1 - me, REACH))

    for d in OFFSETS:

        @pl.when(valid(d))
        def _():
            for a in range(count):
                copy(a, d, ins[a], REACH - d).start()

    for a in range(count):
        outs[a][REACH] = ins[a][...]
    for d in OFFSETS:

        @pl.when(jnp.logical_not(valid(d)))
        def _():
            for a in range(count):
                outs[a][REACH + d] = jnp.zeros(ins[a].shape, ins[a].dtype)

    for d in OFFSETS:

        @pl.when(valid(d))
        def _():
            for a in range(count):
                copy(a, d, ins[a], REACH - d).wait_send()
                copy(a, d, ins[a], REACH + d).wait_recv()


def halo(collective_id, *arrays):
    count = len(arrays)
    return pl.pallas_call(
        functools.partial(halo_kernel, count),
        out_shape=[jax.ShapeDtypeStruct((SLOTS,) + a.shape, a.dtype) for a in arrays],
        in_specs=[VMEM] * count,
        out_specs=[VMEM] * count,
        scratch_shapes=[
            pltpu.SemaphoreType.DMA((count, SLOTS)),
            pltpu.SemaphoreType.DMA((count, SLOTS)),
        ],
        compiler_params=pltpu.CompilerParams(
            collective_id=collective_id, has_side_effects=True, vmem_limit_bytes=LIMIT
        ),
    )(*arrays)


def gather_halo_kernel(count, *refs):
    n = lax.axis_size("enc")
    pieces, ins, fulls = refs[:2], refs[2 : 2 + count], refs[2 + count : 4 + count]
    outs = refs[4 + count : 4 + 2 * count]
    send, recv, shard_send, shard_recv = refs[4 + 2 * count :]
    me, group = lax.axis_index("enc"), lax.axis_index("groups")
    half = pieces[0].shape[1] // 2
    barrier = pltpu.get_barrier_semaphore()
    planes = n // 4
    z = me // 4
    across = me + 2 - 4 * (lax.rem(me, 4) // 2)
    other = me + 1 - 2 * lax.rem(me, 2)
    sent = []

    def valid(d):
        return me + d < n if d > 0 else me + d >= 0

    def present(*steps):
        good = z >= 0
        for step in steps:
            good = jnp.logical_and(good, z + step < planes if step > 0 else z + step >= 0)
        return good

    def copy(a, d, source, slot):
        return pltpu.make_async_remote_copy(
            src_ref=source,
            dst_ref=outs[a].at[slot],
            send_sem=send.at[a, REACH + d],
            recv_sem=recv.at[a, slot],
            device_id={"enc": me + d},
            device_id_type=MESH,
        )

    def shard(s, part, k, device, source=None):
        layer, piece = part
        columns = pl.ds(pl.multiple_of(piece * half, half), half)
        dst, unit = fulls[layer].at[s, :, columns], 2 * layer + piece
        if source is not None:
            source = source.at[:, columns]
        return pltpu.make_async_remote_copy(
            src_ref=dst if source is None else source,
            dst_ref=dst,
            send_sem=shard_send.at[s, unit, k],
            recv_sem=shard_recv.at[s, unit],
            device_id=device,
            device_id_type=MESH,
        )

    core, side, twin = {"enc": other}, {"enc": across}, {"groups": 1 - group}

    def begin(steps, s, part, k, device, source=None):
        sent.append((steps, s, part, k, device, source))

        @pl.when(present(*steps))
        def _():
            shard(s, part, k, device, source).start()

    def arrive(steps, s, part):
        @pl.when(present(*steps))
        def _():
            shard(s, part, 3, core).wait_recv()

    for d in OFFSETS:

        @pl.when(valid(d))
        def _():
            pl.semaphore_signal(barrier, inc=1, device_id={"enc": me + d}, device_id_type=MESH)

    pl.semaphore_signal(barrier, inc=1, device_id=twin, device_id_type=MESH)
    pl.semaphore_wait(barrier, jnp.minimum(me, REACH) + jnp.minimum(n - 1 - me, REACH) + 1)

    for layer, piece in enumerate(pieces):
        part = (layer, group)
        begin((1,), me, part, 0, {"enc": me + 4}, piece)
        begin((-1,), me, part, 1, {"enc": me - 4}, piece)
        begin((), me, part, 2, side, piece)
        begin((), me, part, 3, core, piece)
        begin((), me, (layer, 1 - group), 3, core, piece)
    for d in OFFSETS:

        @pl.when(valid(d))
        def _():
            for a in range(count):
                copy(a, d, ins[a], REACH - d).start()

    for f in range(2):
        fulls[f][me] = pieces[f][...]
    for a in range(count):
        outs[a][REACH] = ins[a][...]
    for d in OFFSETS:

        @pl.when(jnp.logical_not(valid(d)))
        def _():
            for a in range(count):
                outs[a][REACH + d] = jnp.zeros(ins[a].shape, ins[a].dtype)

    def steps_at(distance):
        return sorted({-distance, distance}) if 0 <= distance < planes else []

    for distance in range(1, planes + 2):
        for part in ((0, group), (1, group)):
            for step in steps_at(distance):
                s, back = me + 4 * step, -1 if step > 0 else 1
                arrive((step,), s, part)
                begin((step, back), s, part, 0, {"enc": me + 4 * back})
                begin((step,), s, part, 2, side)
                begin((step,), s, part, 3, core)
                begin((step,), s, part, 4, twin)
        for part in ((0, group), (1, group)):
            for step in steps_at(distance - 1):
                s = across + 4 * step
                arrive((step,), s, part)
                begin((step,), s, part, 3, core)
                begin((step,), s, part, 4, twin)
        lines = [(step, me + 4 * step) for step in steps_at(distance - 1) if step]
        lines += [(step, across + 4 * step) for step in steps_at(distance - 2)]
        for layer in range(2):
            for step, s in lines:
                arrive((step,), s, (layer, 1 - group))
                begin((step,), s, (layer, 1 - group), 3, core)

    for plane in range(planes):
        for x in range(2):
            s = 4 * plane + 2 * x + lax.rem(other, 2)
            for part in ((0, 0), (0, 1), (1, 0), (1, 1)):
                arrive((), s, part)

    for d in OFFSETS:

        @pl.when(valid(d))
        def _():
            for a in range(count):
                copy(a, d, ins[a], REACH - d).wait_send()
                copy(a, d, ins[a], REACH + d).wait_recv()

    for steps, *rest in sent:

        @pl.when(present(*steps))
        def _():
            shard(*rest).wait_send()


def gather_halo(pieces, *arrays):
    count = len(arrays)
    n = lax.axis_size("enc")
    return pl.pallas_call(
        functools.partial(gather_halo_kernel, count),
        out_shape=[jax.ShapeDtypeStruct((n,) + p.shape, p.dtype) for p in pieces]
        + [jax.ShapeDtypeStruct((SLOTS,) + a.shape, a.dtype) for a in arrays],
        in_specs=[VMEM] * (count + 2),
        out_specs=[VMEM] * (count + 2),
        scratch_shapes=[
            pltpu.SemaphoreType.DMA((count, SLOTS)),
            pltpu.SemaphoreType.DMA((count, SLOTS)),
            pltpu.SemaphoreType.DMA((n, 4, 5)),
            pltpu.SemaphoreType.DMA((n, 4)),
        ],
        compiler_params=pltpu.CompilerParams(
            collective_id=0, has_side_effects=True, vmem_limit_bytes=LIMIT
        ),
    )(*pieces, *arrays)


def total_kernel(row_ref, out_ref, held, send, recv):
    n, m = lax.axis_size("enc"), lax.axis_size("dp")
    total = n * m
    me = lax.axis_index("enc") * m + lax.axis_index("dp")
    barrier = pltpu.get_barrier_semaphore()

    def peer(o):
        t = lax.rem(me + o, total)
        return {"enc": t // m, "dp": lax.rem(t, m)}

    def copy(o):
        return pltpu.make_async_remote_copy(
            src_ref=row_ref,
            dst_ref=held.at[o],
            send_sem=send.at[o],
            recv_sem=recv.at[o],
            device_id=peer(o),
            device_id_type=MESH,
        )

    def greet(o, c):
        pl.semaphore_signal(barrier, inc=1, device_id=peer(o), device_id_type=MESH)
        return c

    def begin(o, c):
        copy(o).start()
        return c

    def finish(o, c):
        copy(o).wait()
        return c

    lax.fori_loop(1, total, greet, 0)
    pl.semaphore_wait(barrier, total - 1)
    lax.fori_loop(1, total, begin, 0)
    held[0] = row_ref[...]
    lax.fori_loop(1, total, finish, 0)

    out_ref[...] = lax.fori_loop(1, total, lambda o, s: s + held[o], held[0])


def total_rows(rows):
    total = lax.axis_size("enc") * lax.axis_size("dp")
    return pl.pallas_call(
        total_kernel,
        out_shape=jax.ShapeDtypeStruct(rows.shape, rows.dtype),
        in_specs=[VMEM],
        out_specs=VMEM,
        scratch_shapes=[
            pltpu.VMEM((total,) + rows.shape, rows.dtype),
            pltpu.SemaphoreType.DMA((total,)),
            pltpu.SemaphoreType.DMA((total,)),
        ],
        compiler_params=pltpu.CompilerParams(
            collective_id=2, has_side_effects=True, vmem_limit_bytes=LIMIT
        ),
    )(rows)


def first_slot(tags):
    first = REACH
    for s in range(REACH - 1, -1, -1):
        first = jnp.where(tags[s] == tags[REACH], s, first)
    return first


def band_mask(tags, first, band):
    lanes = lax.broadcasted_iota(jnp.int32, (1, MAXB * band), 1)
    mask = lanes < 0
    for j in range(MAXB):
        same = (tags[first + j] == tags[REACH]).astype(jnp.int32)
        inside = jnp.logical_and(lanes >= j * band, lanes < (j + 1) * band)
        mask = jnp.logical_or(mask, jnp.logical_and(inside, same == 1))
    return mask


def full_kernel(tags, near, weight, gain, packed, att, lse, hidden):
    band = near.shape[1]
    cols = HEADS * HDIM
    first = first_slot(tags)
    mask = band_mask(tags, first, band)
    for j in range(MAXB):
        x = near[first + j].astype(F32)
        normed, _ = normalize(x, gain[0:1, :])
        for c in range(3):
            packed[j * band : (j + 1) * band, c * cols : (c + 1) * cols] = mm(
                normed, weight[:, c * cols : (c + 1) * cols]
            ).astype(BF16)
    own = pl.ds(pl.multiple_of((REACH - first) * band, band), band)
    queries = packed[own, 0:cols]
    lses = []
    for h in range(HEADS):
        a, b = h * HDIM, (h + 1) * HDIM
        scores = mt(queries[:, a:b], packed[:, cols + a : cols + b]) * FACTOR
        scores = jnp.where(mask, scores, MASKED)
        largest = jnp.max(scores, axis=-1, keepdims=True)
        raw = jnp.exp(scores - largest)
        summed = jnp.sum(raw, axis=-1, keepdims=True)
        probs = (raw * (1.0 / summed)).astype(BF16)
        att[:, a:b] = mm(probs, packed[:, 2 * cols + a : 2 * cols + b]).astype(BF16)
        lses.append(largest + jnp.log(summed))
    lse[...] = jnp.concatenate(lses, axis=1)
    hidden[...] = (near[REACH].astype(F32) + mt(att[...], weight[:, 3 * cols :])).astype(BF16)


def window_kernel(
    hidden_ref, cot_ref, same, weight, full_out, gain, att_full, lse_full,
    mixed, dhidden_ref, dout_full, stats, gain_row, packed, att, dpacked,
):
    cols = HEADS * HDIM
    x = hidden_ref[...].astype(F32)
    normed, inverse = normalize(x, gain[1:2, :])
    for c in range(3):
        packed[:, c * cols : (c + 1) * cols] = mm(
            normed, weight[:, c * cols : (c + 1) * cols]
        ).astype(BF16)
    cot = cot_ref[...]
    out_t = weight[:, 3 * cols :]
    dout = mm(cot, out_t).astype(BF16)
    mask = same[...] > 0.5
    for h in range(HEADS):
        a, b = h * HDIM, (h + 1) * HDIM
        q, k = packed[:, a:b], packed[:, cols + a : cols + b]
        v, g = packed[:, 2 * cols + a : 2 * cols + b], dout[:, a:b]
        scores = jnp.where(mask, mt(q, k) * FACTOR, MASKED)
        largest = jnp.max(scores, axis=-1, keepdims=True)
        raw = jnp.exp(scores - largest)
        p = raw * (1.0 / jnp.sum(raw, axis=-1, keepdims=True))
        probs = p.astype(BF16)
        out = mm(probs, v).astype(BF16)
        att[:, a:b] = out
        delta = jnp.sum(g.astype(F32) * out.astype(F32), axis=-1, keepdims=True)
        ds = (p * (mt(g, v) - delta)).astype(BF16)
        dpacked[:, a:b] = (mm(ds, k) * FACTOR).astype(BF16)
        dpacked[:, cols + a : cols + b] = (tm(ds, q) * FACTOR).astype(BF16)
        dpacked[:, 2 * cols + a : 2 * cols + b] = tm(probs, g).astype(BF16)
    mixed[...] = (x + mt(att[...], out_t)).astype(BF16)
    dnormed = mt(dpacked[...], weight[:, : 3 * cols])
    part, row = norm_back(x, gain[1:2, :], inverse, dnormed)
    gain_row[...] = row
    dhidden = cot.astype(F32) + part
    dhidden_ref[...] = dhidden
    dfull = mm(dhidden.astype(BF16), full_out[:, 3 * cols :]).astype(BF16)
    dout_full[...] = dfull
    product = dfull.astype(F32) * att_full[...].astype(F32)
    columns = [lse_full[...]] + [
        jnp.sum(product[:, h * HDIM : (h + 1) * HDIM], axis=-1, keepdims=True)
        for h in range(HEADS)
    ]
    columns.append(jnp.zeros((x.shape[0], 128 - 2 * HEADS), F32))
    stats[...] = jnp.concatenate(columns, axis=1).T[: 2 * HEADS]


def back_kernel(
    tags, packed, near_dout, near_stats, tokens, dhidden, weight, gain,
    grad_tokens, gain_row, dpacked,
):
    band = tokens.shape[0]
    cols = HEADS * HDIM
    first = first_slot(tags)
    mask = band_mask(tags, first, band)
    own = pl.ds(pl.multiple_of((REACH - first) * band, band), band)
    mine = packed[own, :]
    own_stats = near_stats[REACH].T
    gout = jnp.concatenate([near_dout[first + j] for j in range(MAXB)], axis=0)
    rows = jnp.concatenate([near_stats[first + j] for j in range(MAXB)], axis=1)
    own_out = near_dout[REACH]
    for h in range(HEADS):
        a, b = h * HDIM, (h + 1) * HDIM
        q, k, v = mine[:, a:b], mine[:, cols + a : cols + b], mine[:, 2 * cols + a : 2 * cols + b]
        g = own_out[:, a:b]
        near_q = packed[:, a:b]
        near_k = packed[:, cols + a : cols + b]
        near_v = packed[:, 2 * cols + a : 2 * cols + b]
        near_g = gout[:, a:b]
        scores = jnp.where(mask, mt(q, near_k) * FACTOR, MASKED)
        p = jnp.exp(scores - own_stats[:, h : h + 1])
        ds = (p * (mt(g, near_v) - own_stats[:, HEADS + h : HEADS + h + 1])).astype(BF16)
        dpacked[:, a:b] = (mm(ds, near_k) * FACTOR).astype(BF16)
        scores_t = jnp.where(mask, mt(k, near_q) * FACTOR - rows[h : h + 1, :], MASKED)
        pt = jnp.exp(scores_t)
        dst = (pt * (mt(v, near_g) - rows[HEADS + h : HEADS + h + 1, :])).astype(BF16)
        dpacked[:, cols + a : cols + b] = (mm(dst, near_q) * FACTOR).astype(BF16)
        dpacked[:, 2 * cols + a : 2 * cols + b] = mm(pt.astype(BF16), near_g).astype(BF16)
    dnormed = mt(dpacked[...], weight[:, : 3 * cols])
    x = tokens[...].astype(F32)
    inverse = lax.rsqrt(jnp.mean(x * x, axis=-1, keepdims=True) + EPSILON)
    part, row = norm_back(x, gain[0:1, :], inverse, dnormed)
    gain_row[...] = row
    grad_tokens[...] = dhidden[...] + part


def call(kernel, shapes, in_specs, scratch, flops, *args):
    return pl.pallas_call(
        kernel,
        out_shape=[jax.ShapeDtypeStruct(s, t) for s, t in shapes],
        in_specs=in_specs,
        out_specs=[VMEM] * len(shapes),
        scratch_shapes=scratch,
        compiler_params=pltpu.CompilerParams(vmem_limit_bytes=LIMIT),
        cost_estimate=pl.CostEstimate(flops=flops, bytes_accessed=8 << 20, transcendentals=1 << 20),
    )(*args)


def shards(tokens, cotangent, page_of_band, window_order, qkv_weight, out_weight, norm_gain):
    x = tokens[0]
    band, width = x.shape
    cols = HEADS * HDIM
    wide = 3 * cols
    pieces = [jnp.concatenate([qkv_weight[i], out_weight[i].T], axis=1) for i in range(2)]
    tag = jnp.broadcast_to((page_of_band + 1).astype(F32), (8, 128))
    gathers = lax.axis_size("dp") == 1 and lax.axis_size("groups") == 2
    gathers = gathers and lax.axis_size("enc") % 4 == 0 and pieces[0].shape[0] % 16 == 0
    if gathers:
        *fulls, near, near_tag = gather_halo(pieces, x, tag)
        weights = [full.reshape(width, full.shape[2]) for full in fulls]
    else:
        weights = [lax.all_gather(p, ("enc", "dp"), axis=0, tiled=True) for p in pieces]
        near, near_tag = halo(0, x, tag)
    tags = near_tag[:, 0, 0].astype(jnp.int32)
    order = window_order[0, 0]
    late = jnp.arange(band)[:, None] >= WIN
    side = jnp.any((order[:, None] == jnp.arange(band)[None, :]) & late, axis=0)
    same = (side[:, None] == side[None, :]).astype(F32)
    packed, att, lse, hidden = call(
        full_kernel,
        [((MAXB * band, wide), BF16), ((band, cols), BF16), ((band, HEADS), F32), ((band, width), BF16)],
        [SMEM, VMEM, VMEM, VMEM], [], 6 << 30,
        tags, near, weights[0], norm_gain,
    )
    mixed, dhidden, dout, stats, row_window = call(
        window_kernel,
        [((band, width), BF16), ((band, width), F32), ((band, cols), BF16), ((2 * HEADS, band), F32), ((1, width), F32)],
        [VMEM] * 8,
        [pltpu.VMEM((band, wide), BF16), pltpu.VMEM((band, cols), BF16), pltpu.VMEM((band, wide), BF16)],
        3 << 30,
        hidden, cotangent[0], same, weights[1], weights[0], norm_gain, att, lse,
    )
    near_dout, near_stats = halo(1, dout, stats)
    grad_tokens, row_full = call(
        back_kernel,
        [((band, width), F32), ((1, width), F32)],
        [SMEM] + [VMEM] * 7,
        [pltpu.VMEM((band, wide), BF16)],
        3 << 30,
        tags, packed, near_dout, near_stats, x, dhidden, weights[0], norm_gain,
    )
    grad_gain = total_rows(jnp.concatenate([row_full, row_window], axis=0))
    return mixed[None], grad_tokens[None], grad_gain


def solution(mesh):
    return jax.shard_map(
        shards,
        mesh=mesh,
        in_specs=(
            P(("groups", "dp"), "enc", None),
            P(("groups", "dp"), "enc", None),
            P(("groups", "dp"), "enc"),
            P(("groups", "dp"), "enc", None),
            P(None, ("enc", "dp"), None),
            P(None, None, ("enc", "dp")),
            P(),
        ),
        out_specs=(
            P(("groups", "dp"), "enc", None),
            P(("groups", "dp"), "enc", None),
            P("groups", None),
        ),
        check_vma=False,
    )
```
